32 devices in a mesh: node: 8 (over z, x), site: 4 (over y, core).
Axes of the slice: x: 2, y: 2, z: 4, core: 2. Of those that a mesh axis runs over, the one named last changes fastest.
Arguments:
- leaf_partials: float32 [512, 4, 4096], P('node', None, 'site'), may hold values from 0.05 to 1
- dag_edges: int32 [3, 1536, 3], P(None, 'node'), may hold values from 0 to 511, as said below
- weights: float32 [3, 1536], P(None, 'node'), may hold values from 0.25 to 4
- lengths: float32 [3, 1536], P(None, 'node'), may hold values from 0.02 to 2
- counts: int32 [4096], P('site'), may hold values from 1 to 9
- topo_nodes: int32 [32, 8], P('node'), may hold values from 0 to 511
Outputs:
- topology_loglik: float32 [32], P('node')
- edge_gradient: float32 [1536], P('node')
The draws below stay inside these ranges and needn't reach their ends.
Inputs may be any that keep to these rules, and one draw needn't show every extreme that they name: `dag_edges`: in every level each subsplit is the child of exactly 3 edges, listed on the index of node that owns the child; subsplit n is owned by index n // 64. Column 1 is the parent in the next level, column 2 the rotation (0 or 1). Every parent has at least one edge of each rotation. Among the edges of one index of node, at most 32 have parents owned by any one index, and some index receives exactly 32 from every index.
All inputs are finite; a program needn't handle non-finite values.
Results may differ from the reference program's by a relative error of at most 0.0003.
Values sent between devices are 32-bit elements; how exact they have to be, the bound alone decides.
A program may use at most 192 MiB of HBM per device.

```python
import math
import jax
import jax.numpy as jnp
from jax import lax

NODE_DEV = 64
LEVELS = 3
USE = 8
NODES = 512
EDGES = 1536
SITES = 4096
TOPOS = 32
N_NODE = 8


def level_edges(key):
    owners = N_NODE
    node_count = NODE_DEV
    capacity = 4 * node_count // owners
    half_cap = capacity // 2
    busiest = jax.random.randint(jax.random.fold_in(key, 1), (), 0, owners)
    low_keys = jax.random.split(jax.random.fold_in(key, 2), owners)
    low_pairs = jax.vmap(lambda subkey: jax.random.permutation(subkey, 2 * node_count))(low_keys)
    low_pairs = low_pairs.reshape(owners, owners, half_cap).transpose(1, 0, 2)
    high_pairs = jax.random.randint(jax.random.fold_in(key, 3), (owners, owners, half_cap), 0, 2 * node_count)
    pair_table = jnp.concatenate([low_pairs, high_pairs], axis=2).reshape(owners, owners * capacity)
    slot_range = jnp.arange(owners * half_cap)
    high_dest = slot_range // half_cap
    high_slot = high_dest * capacity + half_cap + slot_range % half_cap
    low_slot = slot_range // half_cap * capacity + slot_range % half_cap

    def one_source(source_key, source):
        ranking = jax.random.permutation(jax.random.fold_in(source_key, 1), owners * half_cap)
        priority = ranking + (high_dest != busiest).astype(jnp.int32) * (owners * half_cap)
        picked_slots = jnp.argsort(priority)[:node_count]
        used_slots = jnp.concatenate([low_slot, high_slot[picked_slots]])
        pair_codes = pair_table[source][used_slots]
        destination = used_slots // capacity
        parents = destination * node_count + pair_codes // 2
        rotation = pair_codes % 2
        children = source * node_count + jax.random.permutation(jax.random.fold_in(source_key, 2), jnp.repeat(jnp.arange(node_count), 3))
        shuffle = jax.random.permutation(jax.random.fold_in(source_key, 3), 3 * node_count)
        return jnp.stack([children, parents[shuffle], rotation[shuffle]], axis=1)
    source_keys = jax.random.split(jax.random.fold_in(key, 4), owners)
    return jax.vmap(one_source)(source_keys, jnp.arange(owners)).reshape(owners * 3 * node_count, 3)


def draw_dag_edges(key, part):
    level_keys = jax.random.split(jax.random.fold_in(key, 7), LEVELS)
    return jax.vmap(level_edges)(level_keys).astype(jnp.int32)


def plant(drawn, own_key, low, top_value):
    extent = drawn.shape
    place = [jax.random.randint(jax.random.fold_in(own_key, axis), (), 0, extent[axis]) for axis in range(len(extent))]
    drawn = drawn.at[tuple(place)].set(low)
    longest = extent.index(max(extent))
    place[longest] = (place[longest] + 1) % extent[longest]
    return drawn.at[tuple(place)].set(top_value)


def level_of(key, extent, shards, least, high):
    def one(axis_at, parts):
        steps = jax.random.uniform(jax.random.fold_in(jax.random.fold_in(key, 6), axis_at), (parts,), jnp.float32, least / len(shards), high / len(shards))
        return jnp.repeat(jnp.exp(steps), extent[axis_at] // parts).reshape((-1,) + (1,) * (len(extent) - axis_at - 1))

    loudness = one(*shards[0])
    for cut in shards[1:]:
        loudness = loudness * one(*cut)
    return loudness


def setup_inputs(seed: int = 0) -> dict:
    key_list = jax.random.split(jax.random.key(seed), 7)
    leaf_partials = jnp.clip(0.05 + 0.95 * jax.random.uniform(key_list[0], (NODES, 4, SITES), jnp.float32) ** level_of(key_list[0], (NODES, 4, SITES), ((0, 8), (2, 4)), -0.2, 0.2), 0.05, 1.0)
    dag_edges = draw_dag_edges(jax.random.fold_in(key_list[6], 71), 0)
    weights = jnp.clip(jnp.exp(math.log(4.0) - 2.7725887 * jax.random.uniform(key_list[2], (LEVELS, EDGES), jnp.float32) ** level_of(key_list[2], (LEVELS, EDGES), ((1, 8),), -0.2, 0.2)), 0.25, 4.0)
    lengths = jnp.clip(jnp.exp(math.log(2.0) - 4.6051702 * jax.random.uniform(key_list[3], (LEVELS, EDGES), jnp.float32) ** level_of(key_list[3], (LEVELS, EDGES), ((1, 8),), -0.2, 0.2)), 0.02, 2.0)
    counts = plant(jax.random.randint(key_list[4], (SITES,), 1, 10), jax.random.fold_in(key_list[4], 1), 1, 9).astype(jnp.int32)
    topo_nodes = plant(jax.random.randint(key_list[5], (TOPOS, USE), 0, NODES), jax.random.fold_in(key_list[5], 1), 0, NODES - 1).astype(jnp.int32)
    return {"leaf_partials": leaf_partials, "dag_edges": dag_edges, "weights": weights, "lengths": lengths, "counts": counts, "topo_nodes": topo_nodes}


def transit(child_rows, branch):
    survival = jnp.exp(branch * (-4.0 / 3.0))[:, None, None]
    return survival * child_rows + (1.0 - survival) * 0.25 * jnp.sum(child_rows, axis=1, keepdims=True)


def block_terms(leaf_block, count_block, dag_edges, weights, lengths):
    current = leaf_block
    span = leaf_block.shape[2]
    for level_index in range(LEVELS):
        child_index = dag_edges[level_index, :, 0]
        pair_code = dag_edges[level_index, :, 1] * 2 + dag_edges[level_index, :, 2]
        message = transit(current[child_index], lengths[level_index])
        summed = jax.ops.segment_sum(weights[level_index][:, None, None] * message, pair_code, num_segments=2 * NODES)
        pair_sums = summed.reshape(NODES, 2, 4, span)
        current = pair_sums[:, 0] * pair_sums[:, 1]
    denominator = 0.25 * jnp.sum(current, axis=1)
    scaled = count_block.astype(jnp.float32) / SITES
    node_terms = jnp.sum(scaled[None, :] * jnp.log(denominator), axis=1)
    adjoint = pair_sums[:, ::-1] * (scaled[None, :] * 0.25 / denominator)[:, None, None, :]
    adjoint_rows = adjoint.reshape(2 * NODES, 4, span)[pair_code]
    edge_terms = jnp.sum(message * adjoint_rows, axis=(1, 2))
    return node_terms, edge_terms


def reference(leaf_partials, dag_edges, weights, lengths, counts, topo_nodes):
    site_block = math.gcd(SITES, 512)
    blocks = SITES // site_block
    leaf_blocks = jnp.moveaxis(leaf_partials.reshape(NODES, 4, blocks, site_block), 2, 0)
    count_blocks = counts.reshape(blocks, site_block)

    def one_block(inputs):
        return block_terms(inputs[0], inputs[1], dag_edges, weights, lengths)

    node_parts, edge_parts = lax.map(one_block, (leaf_blocks, count_blocks))
    node_scores = jnp.sum(node_parts, axis=0)
    edge_scores = jnp.sum(edge_parts, axis=0)
    multiplicity = jax.ops.segment_sum(jnp.ones((TOPOS * USE,), jnp.float32), topo_nodes.reshape(-1), num_segments=NODES)
    topology_loglik = jnp.sum(node_scores[topo_nodes], axis=1)
    edge_gradient = multiplicity[dag_edges[LEVELS - 1, :, 1]] * edge_scores
    return topology_loglik, edge_gradient
```

```python
import functools

import jax
import jax.numpy as jnp
from jax import lax
from jax.experimental import pallas as pl
from jax.experimental.pallas import tpu as pltpu
from jax.sharding import PartitionSpec as P


def transit(child_rows, branch):
    survival = jnp.exp(branch * (-4.0 / 3.0))[:, None, None]
    return survival * child_rows + (1.0 - survival) * 0.25 * jnp.sum(
        child_rows, axis=1, keepdims=True
    )


def on_device(leaf_partials, dag_edges, weights, lengths, counts, topo_nodes):
    node_dev, states, site_dev = leaf_partials.shape
    level_count, edge_dev = (dag_edges.shape[0], dag_edges.shape[1])
    owners = lax.axis_size("node")
    device = lax.axis_index("node")
    nodes_all = node_dev * owners
    sites_all = site_dev * lax.axis_size("site")
    scaled = counts.astype(jnp.float32) / sites_all
    incidence = lax.all_gather(topo_nodes, "node", axis=0, tiled=True)
    multiplicity = jax.ops.segment_sum(
        jnp.ones((incidence.size,), jnp.float32), incidence.reshape(-1), num_segments=nodes_all
    )
    capacity = 4 * node_dev // owners
    slots_all = owners * capacity
    current = leaf_partials
    for level_index in range(level_count):
        child_index = dag_edges[level_index, :, 0] - device * node_dev
        parents = dag_edges[level_index, :, 1]
        rotation = dag_edges[level_index, :, 2]
        message = transit(current[child_index], lengths[level_index])
        owner_dev = parents // node_dev
        one_hot = (owner_dev[:, None] == jnp.arange(owners)[None, :]).astype(jnp.int32)
        slot_rank = jnp.sum((jnp.cumsum(one_hot, axis=0) - one_hot) * one_hot, axis=1)
        slot_index = owner_dev * capacity + slot_rank
        pair_code = ((parents - owner_dev * node_dev) * 2 + rotation).astype(jnp.float32)
        buffer = jnp.zeros((slots_all, states, site_dev), jnp.float32).at[slot_index].set(message)
        code_buffer = jnp.full((slots_all,), -1.0, jnp.float32).at[slot_index].set(pair_code)
        weight_buffer = (
            jnp.zeros((slots_all,), jnp.float32).at[slot_index].set(weights[level_index])
        )
        received, received_codes, received_weights = (
            lax.all_to_all(
                buffer.reshape(owners, capacity, states, site_dev),
                "node",
                split_axis=0,
                concat_axis=0,
                tiled=True,
            ),
            lax.all_to_all(
                code_buffer.reshape(owners, capacity),
                "node",
                split_axis=0,
                concat_axis=0,
                tiled=True,
            ),
            lax.all_to_all(
                weight_buffer.reshape(owners, capacity),
                "node",
                split_axis=0,
                concat_axis=0,
                tiled=True,
            ),
        )
        flat_rows = received.reshape(slots_all, states * site_dev)
        selector = (
            received_codes.reshape(-1).astype(jnp.int32)[None, :]
            == jnp.arange(2 * node_dev)[:, None]
        ).astype(jnp.float32)
        summed = jnp.dot(
            selector * received_weights.reshape(-1)[None, :],
            flat_rows,
            precision=lax.Precision.HIGHEST,
            preferred_element_type=jnp.float32,
        )
        pair_sums = summed.reshape(node_dev, 2, states, site_dev)
        current = pair_sums[:, 0] * pair_sums[:, 1]
    denominator = 0.25 * jnp.sum(current, axis=1)
    node_part = jnp.sum(scaled[None, :] * jnp.log(denominator), axis=1)
    adjoint = pair_sums[:, ::-1] * (scaled[None, :] * 0.25 / denominator)[:, None, None, :]
    adjoint_slots = jnp.dot(
        selector.T,
        adjoint.reshape(2 * node_dev, states * site_dev),
        precision=lax.Precision.HIGHEST,
        preferred_element_type=jnp.float32,
    )
    grad_part = jnp.sum(flat_rows * adjoint_slots, axis=1)
    node_scores, slot_grads = lax.psum((node_part, grad_part), "site")
    own_mult = lax.dynamic_slice_in_dim(multiplicity, device * node_dev, node_dev)
    pair_mult = jnp.repeat(own_mult, 2)
    slot_mult = jnp.dot(
        selector.T, pair_mult, precision=lax.Precision.HIGHEST, preferred_element_type=jnp.float32
    )
    returned = lax.all_to_all(
        (slot_grads * slot_mult).reshape(owners, capacity),
        "node",
        split_axis=0,
        concat_axis=0,
        tiled=True,
    )
    edge_gradient = returned.reshape(-1)[slot_index]
    score_table = lax.all_gather(node_scores, "node", axis=0, tiled=True)
    topology_loglik = jnp.sum(score_table[topo_nodes], axis=1)
    return (topology_loglik, edge_gradient)


MESH = pl.DeviceIdType.MESH
F32 = jnp.float32
BF16 = jnp.bfloat16
ROW = 256
SIDE = 128


def halves(x):
    hi = x.astype(BF16)
    return hi, (x - hi.astype(F32)).astype(BF16)


def mm(a, b):
    return jnp.dot(a, b, preferred_element_type=F32)


def mm_nt(a, b):
    return lax.dot_general(a, b, (((1,), (1,)), ((), ())), preferred_element_type=F32)


def kernel(
    dims,
    leaf,
    meta,
    scaled,
    out,
    inbox,
    tables,
    m1h,
    m1l,
    m2h,
    m2l,
    picks,
    gmat,
    chi,
    clo,
    shi,
    slo,
    cur,
    pair,
    ahi,
    alo,
    shadj_hi,
    shadj_lo,
    dst,
    mult,
    send1,
    recv1,
    send2,
    recv2,
    leaf_send,
    leaf_recv,
    meta_send,
    meta_recv,
    own_sem,
    r1_send,
    r1_recv,
    r2_send,
    r2_recv,
):
    owners, site_ways, node_dev, states, levels, topo_here = dims
    nodes = owners * node_dev
    me = lax.axis_index("node")
    my_site = lax.axis_index("site")

    barrier = pltpu.get_barrier_semaphore()
    for i in range(1, owners):
        pl.semaphore_signal(
            barrier, inc=1, device_id={"node": lax.rem(me + i, owners)}, device_id_type=MESH
        )
    for i in range(1, site_ways):
        pl.semaphore_signal(
            barrier, inc=1, device_id={"site": lax.rem(my_site + i, site_ways)}, device_id_type=MESH
        )
    pl.semaphore_wait(barrier, owners - 1 + site_ways - 1)

    meta_copies, leaf_copies = [], []
    for i in range(1, owners):
        copy = pltpu.make_async_remote_copy(
            src_ref=meta,
            dst_ref=tables.at[i],
            send_sem=meta_send.at[i],
            recv_sem=meta_recv.at[i],
            device_id={"node": lax.rem(me + i, owners)},
            device_id_type=MESH,
        )
        copy.start()
        meta_copies.append(copy)
    own_meta = pltpu.make_async_copy(meta, tables.at[0], own_sem.at[0])
    own_meta.start()
    for i in range(1, owners):
        target = lax.rem(me + i, owners)
        copy = pltpu.make_async_remote_copy(
            src_ref=leaf.at[:, :, pl.ds(pl.multiple_of(target * SIDE, SIDE), SIDE)],
            dst_ref=inbox.at[i],
            send_sem=leaf_send.at[i],
            recv_sem=leaf_recv.at[i],
            device_id={"node": target},
            device_id_type=MESH,
        )
        copy.start()
        leaf_copies.append(copy)
    own_leaf = pltpu.make_async_copy(
        leaf.at[:, :, pl.ds(pl.multiple_of(me * SIDE, SIDE), SIDE)], inbox.at[0], own_sem.at[1]
    )
    own_leaf.start()

    own_meta.wait()
    for copy in meta_copies:
        copy.wait_recv()

    def absolute(first, rows):
        row = lax.broadcasted_iota(jnp.int32, (rows, SIDE), 0) + first
        node = lax.rem(row, nodes)
        owner = lax.rem(me - node // node_dev + owners, owners)
        code = (row // nodes) * nodes + owner * node_dev + lax.rem(node, node_dev)
        return code.astype(F32)[:, :1]

    lane = lax.broadcasted_iota(jnp.int32, (1, SIDE), 1)
    topo_lane = (lane >= SIDE // 2) & (lane < SIDE // 2 + topo_here)
    child_iota = lax.broadcasted_iota(jnp.int32, (2 * node_dev, ROW), 0).astype(F32)

    chunk = 256

    def build(step, carry):
        level = step // (owners // 2)
        duo = lax.rem(step, owners // 2)
        codes = []
        for a in range(2):
            child = tables[2 * duo + a, level, 0:1, :]
            codes.append(tables[2 * duo + a, level, 1:2, :])
            weight = tables[2 * duo + a, level, 2:3, :]
            q = tables[2 * duo + a, level, 3:4, :]
            hot = child_iota == child + float(a * node_dev)
            g1h, g1l = halves(jnp.where(hot, weight * q, 0.0))
            g2h, g2l = halves(jnp.where(hot, weight * (1.0 - q) * 0.25, 0.0))
            columns = slice(a * ROW, (a + 1) * ROW)
            for n, piece in enumerate((g1h, g1l, g2h, g2l)):
                gmat[n * SIDE : (n + 1) * SIDE, columns] = piece
        code = jnp.concatenate(codes, axis=1)
        where_to = pl.ds(pl.multiple_of(duo * SIDE, SIDE), SIDE)
        for first in range(0, 2 * nodes, chunk):
            pick = jnp.where(absolute(first, chunk) == code, 1.0, 0.0).astype(BF16)
            rows = slice(first, first + chunk)

            @pl.when(level == levels - 1)
            def _():
                picks[duo, rows, :] = pick

            found = mm_nt(pick, gmat[...])
            hi, lo = halves(found[:, :SIDE] + found[:, SIDE : 2 * SIDE])
            m1h[level, rows, where_to] = hi
            m1l[level, rows, where_to] = lo
            hi, lo = halves(found[:, 2 * SIDE : 3 * SIDE] + found[:, 3 * SIDE :])
            m2h[level, rows, where_to] = hi
            m2l[level, rows, where_to] = lo
        return carry

    lax.fori_loop(0, levels * (owners // 2), build, 0)

    node_abs = absolute(0, nodes)
    times = jnp.zeros((nodes, SIDE), F32)
    for i in range(owners):
        wanted = jnp.where(topo_lane, tables[i, levels - 1, 0:1, SIDE:], -1.0)
        times += jnp.where(node_abs == wanted, 1.0, 0.0)
    mult[...] = jnp.broadcast_to(jnp.sum(times, axis=1, keepdims=True), (nodes, SIDE))

    own_leaf.wait()
    for i in range(owners):
        if i:
            leaf_copies[i - 1].wait_recv()
        block = inbox[i]
        rows = slice(i * node_dev, (i + 1) * node_dev)
        for k in range(states):
            cur[rows, k * SIDE : (k + 1) * SIDE] = block[:, k, :]

    def split(first, carry):
        rows = pl.ds(pl.multiple_of(first * SIDE, SIDE), SIDE)
        x = cur[rows, :]
        chi[rows, :], clo[rows, :] = halves(x)
        total = x[:, :SIDE]
        for k in range(1, states):
            total = total + x[:, k * SIDE : (k + 1) * SIDE]
        shi[rows, :], slo[rows, :] = halves(total)
        return carry

    for level in range(levels):
        lax.fori_loop(0, nodes // SIDE, split, 0)

        def advance(step, carry, level=level):
            rows = pl.ds(pl.multiple_of(step * SIDE, SIDE), SIDE)
            made = []
            for r in range(2):
                source = pl.ds(pl.multiple_of(r * nodes + step * SIDE, SIDE), SIDE)
                ah, al = m1h[level, source, :], m1l[level, source, :]
                bh, bl = m2h[level, source, :], m2l[level, source, :]
                flat = mm(bh, shi[...]) + mm(bh, slo[...]) + mm(bl, shi[...])
                full = mm(ah, chi[...]) + mm(ah, clo[...]) + mm(al, chi[...])
                made.append(full + jnp.concatenate([flat] * states, axis=1))
                if level == levels - 1:
                    pair[source, :] = made[r]
            cur[rows, :] = made[0] * made[1]
            return carry

        lax.fori_loop(0, nodes // SIDE, advance, 0)

    site_row = lax.broadcasted_iota(jnp.int32, scaled.shape, 0)
    count = jnp.sum(jnp.where(site_row == me, scaled[...], 0.0), axis=0, keepdims=True)
    picked = [jnp.zeros((1, SIDE), F32)] * owners
    for first in range(0, nodes, SIDE):
        rows = slice(first, first + SIDE)
        x = cur[rows, :]
        total = x[:, :SIDE]
        for k in range(1, states):
            total = total + x[:, k * SIDE : (k + 1) * SIDE]
        lik = 0.25 * total
        score = jnp.sum(count * jnp.log(lik), axis=1, keepdims=True)
        here = absolute(first, SIDE)
        for i in range(owners):
            wanted = jnp.where(topo_lane, tables[i, levels - 1, 0:1, SIDE:], -1.0)
            picked[i] = picked[i] + jnp.sum(
                jnp.where(here == wanted, score, 0.0), axis=0, keepdims=True
            )
        factor = count * 0.25 / lik * mult[rows, :]
        wide = jnp.concatenate([factor] * states, axis=1)
        for r in range(2):
            adj = pair[(1 - r) * nodes + first : (1 - r) * nodes + first + SIDE, :] * wide
            to = slice(r * nodes + first, r * nodes + first + SIDE)
            ahi[to, :], alo[to, :] = halves(adj)
            flat = adj[:, :SIDE]
            for k in range(1, states):
                flat = flat + adj[:, k * SIDE : (k + 1) * SIDE]
            shadj_hi[to, :], shadj_lo[to, :] = halves(flat)

    def products(step, carry):
        cols = pl.ds(pl.multiple_of(step * ROW, ROW), ROW)
        ah, al = ahi[cols, :], alo[cols, :]
        sh, sl = shadj_hi[cols, :], shadj_lo[cols, :]
        d1 = mm_nt(chi[...], ah) + mm_nt(chi[...], al) + mm_nt(clo[...], ah)
        d2 = mm_nt(shi[...], sh) + mm_nt(shi[...], sl) + mm_nt(slo[...], sh)
        d1h, d1l = halves(d1)
        d2h, d2l = halves(d2)
        for i in range(owners):
            rows = slice(i * node_dev, (i + 1) * node_dev)
            for n, piece in enumerate((d1h, d1l, d2h, d2l)):
                dst[i, n * node_dev : (n + 1) * node_dev, cols] = piece[rows, :]
        return carry

    lax.fori_loop(0, 2 * nodes // ROW, products, 0)

    edge_iota = lax.broadcasted_iota(jnp.int32, (node_dev, ROW), 0).astype(F32)
    last = levels - 1
    for i in range(owners):
        found = mm(dst[i], picks[i // 2, :, (i % 2) * ROW : (i % 2 + 1) * ROW])
        hot = edge_iota == tables[i, last, 0:1, :]
        d1 = found[:node_dev] + found[node_dev : 2 * node_dev]
        d2 = found[2 * node_dev : 3 * node_dev] + found[3 * node_dev :]
        q = tables[i, last, 3:4, :]
        mixed = jnp.where(hot, q * d1 + (1.0 - q) * 0.25 * d2, 0.0)
        grads = jnp.sum(mixed, axis=0, keepdims=True)
        grads = grads + jnp.concatenate([jnp.zeros((1, SIDE), F32), picked[i]], axis=1)
        send1[i] = jnp.broadcast_to(grads, (8, ROW))

    first_copies = []
    for i in range(1, owners):
        copy = pltpu.make_async_remote_copy(
            src_ref=send1.at[i],
            dst_ref=recv1.at[i],
            send_sem=r1_send.at[i],
            recv_sem=r1_recv.at[i],
            device_id={"node": lax.rem(me - i + owners, owners)},
            device_id_type=MESH,
        )
        copy.start()
        first_copies.append(copy)
    total = send1[0]
    for i in range(1, owners):
        first_copies[i - 1].wait_recv()
        total = total + recv1[i]
    send2[...] = total
    recv2[my_site] = total
    second_copies = []
    for i in range(1, site_ways):
        copy = pltpu.make_async_remote_copy(
            src_ref=send2,
            dst_ref=recv2.at[my_site],
            send_sem=r2_send.at[i],
            recv_sem=r2_recv.at[i],
            device_id={"site": lax.rem(my_site + i, site_ways)},
            device_id_type=MESH,
        )
        copy.start()
        second_copies.append(copy)
    for copy in second_copies:
        copy.wait_recv()
    total = recv2[0]
    for i in range(1, site_ways):
        total = total + recv2[i]
    out[...] = total
    for copy in meta_copies + leaf_copies + first_copies + second_copies:
        copy.wait_send()


def by_sites(leaf_partials, dag_edges, weights, lengths, counts, topo_nodes):
    node_dev, states, site_dev = leaf_partials.shape
    levels, edge_dev, _ = dag_edges.shape
    owners, site_ways = lax.axis_size("node"), lax.axis_size("site")
    nodes = owners * node_dev
    topo_here = topo_nodes.size
    edges = jnp.transpose(dag_edges, (2, 0, 1))
    child = edges[0] - lax.axis_index("node") * node_dev
    code = edges[2] * nodes + edges[1]
    tail = ROW - edge_dev
    extra = jnp.pad(topo_nodes.reshape(-1), (0, tail - topo_here))
    child = jnp.concatenate([child, jnp.broadcast_to(extra, (levels, tail))], axis=1)
    pad = ((0, 0), (0, tail))
    meta = jnp.stack(
        [
            child.astype(F32),
            jnp.pad(code, pad, constant_values=-1).astype(F32),
            jnp.pad(weights, pad),
            jnp.pad(jnp.exp(lengths * (-4.0 / 3.0)), pad),
        ],
        axis=1,
    )
    scaled = (counts.astype(F32) / (site_dev * site_ways)).reshape(owners, SIDE)
    wide = states * SIDE
    out = pl.pallas_call(
        functools.partial(
            kernel, (owners, site_ways, node_dev, states, levels, topo_here)
        ),
        out_shape=jax.ShapeDtypeStruct((8, ROW), F32),
        in_specs=[
            pl.BlockSpec(memory_space=pl.ANY),
            pl.BlockSpec(memory_space=pltpu.VMEM),
            pl.BlockSpec(memory_space=pltpu.VMEM),
        ],
        out_specs=pl.BlockSpec(memory_space=pltpu.VMEM),
        scratch_shapes=[
            pltpu.VMEM((owners, node_dev, states, SIDE), F32),
            pltpu.VMEM((owners, levels, 4, ROW), F32),
            pltpu.VMEM((levels, 2 * nodes, nodes), BF16),
            pltpu.VMEM((levels, 2 * nodes, nodes), BF16),
            pltpu.VMEM((levels, 2 * nodes, nodes), BF16),
            pltpu.VMEM((levels, 2 * nodes, nodes), BF16),
            pltpu.VMEM((owners // 2, 2 * nodes, 2 * ROW), BF16),
            pltpu.VMEM((4 * SIDE, 2 * ROW), BF16),
            pltpu.VMEM((nodes, wide), BF16),
            pltpu.VMEM((nodes, wide), BF16),
            pltpu.VMEM((nodes, SIDE), BF16),
            pltpu.VMEM((nodes, SIDE), BF16),
            pltpu.VMEM((nodes, wide), F32),
            pltpu.VMEM((2 * nodes, wide), F32),
            pltpu.VMEM((2 * nodes, wide), BF16),
            pltpu.VMEM((2 * nodes, wide), BF16),
            pltpu.VMEM((2 * nodes, SIDE), BF16),
            pltpu.VMEM((2 * nodes, SIDE), BF16),
            pltpu.VMEM((owners, 4 * node_dev, 2 * nodes), BF16),
            pltpu.VMEM((nodes, SIDE), F32),
            pltpu.VMEM((owners, 8, ROW), F32),
            pltpu.VMEM((owners, 8, ROW), F32),
            pltpu.VMEM((8, ROW), F32),
            pltpu.VMEM((site_ways, 8, ROW), F32),
            pltpu.SemaphoreType.DMA((owners,)),
            pltpu.SemaphoreType.DMA((owners,)),
            pltpu.SemaphoreType.DMA((owners,)),
            pltpu.SemaphoreType.DMA((owners,)),
            pltpu.SemaphoreType.DMA((2,)),
            pltpu.SemaphoreType.DMA((owners,)),
            pltpu.SemaphoreType.DMA((owners,)),
            pltpu.SemaphoreType.DMA((site_ways,)),
            pltpu.SemaphoreType.DMA((site_ways,)),
        ],
        compiler_params=pltpu.CompilerParams(
            collective_id=0, has_side_effects=True, vmem_limit_bytes=50 * 2**20
        ),
    )(leaf_partials, meta, scaled)
    loglik = jnp.sum(
        out[0, edge_dev : edge_dev + topo_here].reshape(topo_nodes.shape), axis=1
    )
    return loglik, out[0, :edge_dev]


def either(leaf_partials, dag_edges, weights, lengths, counts, topo_nodes):
    node_dev, states, site_dev = leaf_partials.shape
    owners = lax.axis_size("node")
    fits = (
        site_dev == owners * SIDE
        and 2 * node_dev == SIDE
        and owners % 2 == 0
        and owners <= 8
        and dag_edges.shape[1] == ROW * 3 // 4
        and topo_nodes.size <= ROW // 4
    )
    form = by_sites if fits else on_device
    return form(leaf_partials, dag_edges, weights, lengths, counts, topo_nodes)


def solution(mesh):
    return jax.shard_map(
        either,
        mesh=mesh,
        in_specs=(
            P("node", None, "site"),
            P(None, "node", None),
            P(None, "node"),
            P(None, "node"),
            P("site"),
            P("node", None),
        ),
        out_specs=(P("node"), P("node")),
        check_vma=False,
    )
```

```python
import functools

import jax
import jax.numpy as jnp
from jax import lax
from jax.experimental import pallas as pl
from jax.experimental.pallas import tpu as pltpu
from jax.sharding import PartitionSpec as P


def transit(child_rows, branch):
    survival = jnp.exp(branch * (-4.0 / 3.0))[:, None, None]
    return survival * child_rows + (1.0 - survival) * 0.25 * jnp.sum(
        child_rows, axis=1, keepdims=True
    )


def on_device(leaf_partials, dag_edges, weights, lengths, counts, topo_nodes):
    node_dev, states, site_dev = leaf_partials.shape
    level_count, edge_dev = (dag_edges.shape[0], dag_edges.shape[1])
    owners = lax.axis_size("node")
    device = lax.axis_index("node")
    nodes_all = node_dev * owners
    sites_all = site_dev * lax.axis_size("site")
    scaled = counts.astype(jnp.float32) / sites_all
    incidence = lax.all_gather(topo_nodes, "node", axis=0, tiled=True)
    multiplicity = jax.ops.segment_sum(
        jnp.ones((incidence.size,), jnp.float32), incidence.reshape(-1), num_segments=nodes_all
    )
    capacity = 4 * node_dev // owners
    slots_all = owners * capacity
    current = leaf_partials
    for level_index in range(level_count):
        child_index = dag_edges[level_index, :, 0] - device * node_dev
        parents = dag_edges[level_index, :, 1]
        rotation = dag_edges[level_index, :, 2]
        message = transit(current[child_index], lengths[level_index])
        owner_dev = parents // node_dev
        one_hot = (owner_dev[:, None] == jnp.arange(owners)[None, :]).astype(jnp.int32)
        slot_rank = jnp.sum((jnp.cumsum(one_hot, axis=0) - one_hot) * one_hot, axis=1)
        slot_index = owner_dev * capacity + slot_rank
        pair_code = ((parents - owner_dev * node_dev) * 2 + rotation).astype(jnp.float32)
        buffer = jnp.zeros((slots_all, states, site_dev), jnp.float32).at[slot_index].set(message)
        code_buffer = jnp.full((slots_all,), -1.0, jnp.float32).at[slot_index].set(pair_code)
        weight_buffer = (
            jnp.zeros((slots_all,), jnp.float32).at[slot_index].set(weights[level_index])
        )
        received, received_codes, received_weights = (
            lax.all_to_all(
                buffer.reshape(owners, capacity, states, site_dev),
                "node",
                split_axis=0,
                concat_axis=0,
                tiled=True,
            ),
            lax.all_to_all(
                code_buffer.reshape(owners, capacity),
                "node",
                split_axis=0,
                concat_axis=0,
                tiled=True,
            ),
            lax.all_to_all(
                weight_buffer.reshape(owners, capacity),
                "node",
                split_axis=0,
                concat_axis=0,
                tiled=True,
            ),
        )
        flat_rows = received.reshape(slots_all, states * site_dev)
        selector = (
            received_codes.reshape(-1).astype(jnp.int32)[None, :]
            == jnp.arange(2 * node_dev)[:, None]
        ).astype(jnp.float32)
        summed = jnp.dot(
            selector * received_weights.reshape(-1)[None, :],
            flat_rows,
            precision=lax.Precision.HIGHEST,
            preferred_element_type=jnp.float32,
        )
        pair_sums = summed.reshape(node_dev, 2, states, site_dev)
        current = pair_sums[:, 0] * pair_sums[:, 1]
    denominator = 0.25 * jnp.sum(current, axis=1)
    node_part = jnp.sum(scaled[None, :] * jnp.log(denominator), axis=1)
    adjoint = pair_sums[:, ::-1] * (scaled[None, :] * 0.25 / denominator)[:, None, None, :]
    adjoint_slots = jnp.dot(
        selector.T,
        adjoint.reshape(2 * node_dev, states * site_dev),
        precision=lax.Precision.HIGHEST,
        preferred_element_type=jnp.float32,
    )
    grad_part = jnp.sum(flat_rows * adjoint_slots, axis=1)
    node_scores, slot_grads = lax.psum((node_part, grad_part), "site")
    own_mult = lax.dynamic_slice_in_dim(multiplicity, device * node_dev, node_dev)
    pair_mult = jnp.repeat(own_mult, 2)
    slot_mult = jnp.dot(
        selector.T, pair_mult, precision=lax.Precision.HIGHEST, preferred_element_type=jnp.float32
    )
    returned = lax.all_to_all(
        (slot_grads * slot_mult).reshape(owners, capacity),
        "node",
        split_axis=0,
        concat_axis=0,
        tiled=True,
    )
    edge_gradient = returned.reshape(-1)[slot_index]
    score_table = lax.all_gather(node_scores, "node", axis=0, tiled=True)
    topology_loglik = jnp.sum(score_table[topo_nodes], axis=1)
    return (topology_loglik, edge_gradient)


MESH = pl.DeviceIdType.MESH
F32 = jnp.float32
BF16 = jnp.bfloat16
ROW = 256
SIDE = 128


def halves(x):
    hi = x.astype(BF16)
    return hi, (x - hi.astype(F32)).astype(BF16)


def mm(a, b):
    return jnp.dot(a, b, preferred_element_type=F32)


def mm_nt(a, b):
    return lax.dot_general(a, b, (((1,), (1,)), ((), ())), preferred_element_type=F32)


def kernel(
    dims,
    leaf,
    edges_hbm,
    weights_hbm,
    lengths_hbm,
    counts_hbm,
    topo_hbm,
    loglik_out,
    grad_out,
    edges,
    weights,
    lengths,
    counts,
    topo,
    meta,
    inbox,
    tables,
    m1h,
    m1l,
    m2h,
    m2l,
    picks,
    gmat,
    ch,
    cl,
    sums,
    pair,
    lik_sum,
    ahi,
    alo,
    adj_sums,
    dst,
    numbers,
    mult,
    send1,
    recv1,
    send2,
    recv2,
    leaf_send,
    leaf_recv,
    meta_send,
    meta_recv,
    own_sem,
    r1_send,
    r1_recv,
    r2_send,
    r2_recv,
):
    owners, site_ways, node_dev, states, levels, topo_shape, sites_all = dims
    nodes = owners * node_dev
    edge_dev = edges.shape[2]
    topo_here = topo_shape[0] * topo_shape[1]
    me = lax.axis_index("node")
    my_site = lax.axis_index("site")

    small = []
    for n, (a, b) in enumerate(
        (
            (edges_hbm, edges),
            (weights_hbm, weights),
            (lengths_hbm, lengths),
            (counts_hbm, counts),
            (topo_hbm, topo),
        )
    ):
        copy = pltpu.make_async_copy(a, b, own_sem.at[n])
        copy.start()
        small.append(copy)
    own_leaf = pltpu.make_async_copy(
        leaf.at[:, :, pl.ds(pl.multiple_of(me * SIDE, SIDE), SIDE)], inbox.at[0], own_sem.at[5]
    )
    own_leaf.start()

    barrier = pltpu.get_barrier_semaphore()
    for i in range(1, owners):
        pl.semaphore_signal(
            barrier, inc=1, device_id={"node": lax.rem(me + i, owners)}, device_id_type=MESH
        )
    for i in range(1, site_ways):
        pl.semaphore_signal(
            barrier, inc=1, device_id={"site": lax.rem(my_site + i, site_ways)}, device_id_type=MESH
        )

    meta[...] = jnp.full(meta.shape, -1.0, F32)
    for copy in small:
        copy.wait()
    for level in range(levels):
        child = edges[level, 0:1, :] - me * node_dev
        code = edges[level, 2:3, :] * nodes + edges[level, 1:2, :]
        meta[level, 0:1, 0:edge_dev] = child.astype(F32)
        meta[level, 1:2, 0:edge_dev] = code.astype(F32)
        meta[level, 2:3, 0:edge_dev] = weights[level : level + 1, :]
        meta[level, 3:4, 0:edge_dev] = jnp.exp(lengths[level : level + 1, :] * (-4.0 / 3.0))
    for t in range(topo_shape[0]):
        first = edge_dev + t * topo_shape[1]
        meta[levels - 1, 0:1, first : first + topo_shape[1]] = topo[t : t + 1, :].astype(F32)

    pl.semaphore_wait(barrier, owners - 1 + site_ways - 1)

    meta_copies, leaf_copies = [], []
    for i in range(1, owners):
        copy = pltpu.make_async_remote_copy(
            src_ref=meta,
            dst_ref=tables.at[i],
            send_sem=meta_send.at[i],
            recv_sem=meta_recv.at[i],
            device_id={"node": lax.rem(me + i, owners)},
            device_id_type=MESH,
        )
        copy.start()
        meta_copies.append(copy)
    for i in range(1, owners):
        target = lax.rem(me + i, owners)
        copy = pltpu.make_async_remote_copy(
            src_ref=leaf.at[:, :, pl.ds(pl.multiple_of(target * SIDE, SIDE), SIDE)],
            dst_ref=inbox.at[i],
            send_sem=leaf_send.at[i],
            recv_sem=leaf_recv.at[i],
            device_id={"node": target},
            device_id_type=MESH,
        )
        copy.start()
        leaf_copies.append(copy)
    tables[0] = meta[...]

    local = lax.broadcasted_iota(jnp.int32, (node_dev, SIDE), 0)
    for r in range(2):
        for i in range(owners):
            first = r * nodes + i * node_dev
            owner = lax.rem(me - i + owners, owners)
            numbers[first : first + node_dev, :] = (
                local + (r * nodes + owner * node_dev)
            ).astype(F32)

    lane = lax.broadcasted_iota(jnp.int32, (1, SIDE), 1)
    topo_lane = (lane >= SIDE // 2) & (lane < SIDE // 2 + topo_here)
    child_iota = lax.broadcasted_iota(jnp.int32, (2 * node_dev, ROW), 0).astype(F32)

    for copy in meta_copies:
        copy.wait_recv()

    def build(step, carry):
        level = step // (owners // 2)
        duo = lax.rem(step, owners // 2)
        codes = []
        for a in range(2):
            child = tables[2 * duo + a, level, 0:1, :]
            codes.append(tables[2 * duo + a, level, 1:2, :])
            weight = tables[2 * duo + a, level, 2:3, :]
            q = tables[2 * duo + a, level, 3:4, :]
            hot = child_iota == child + float(a * node_dev)
            g1h, g1l = halves(jnp.where(hot, weight * q, 0.0))
            g2h, g2l = halves(jnp.where(hot, weight * (1.0 - q) * 0.25, 0.0))
            columns = slice(a * ROW, (a + 1) * ROW)
            for n, piece in enumerate((g1h, g1l, g2h, g2l)):
                gmat[n * SIDE : (n + 1) * SIDE, columns] = piece
        code = jnp.concatenate(codes, axis=1)

        def choose(part, inner):
            rows = pl.ds(pl.multiple_of(part * SIDE, SIDE), SIDE)
            wide = jnp.concatenate([numbers[rows, :]] * 4, axis=1)
            picks[duo, rows, :] = jnp.where(wide == code, 1.0, 0.0).astype(BF16)
            return inner

        lax.fori_loop(0, 2 * nodes // SIDE, choose, 0)
        where_to = pl.ds(pl.multiple_of(duo * SIDE, SIDE), SIDE)
        for r in range(2):
            rows = slice(r * nodes, (r + 1) * nodes)
            found = mm_nt(picks[duo, rows, :], gmat[0 : 2 * SIDE, :])
            hi, lo = halves(found[:, :SIDE] + found[:, SIDE:])
            m1h[level, rows, where_to] = hi
            m1l[level, rows, where_to] = lo
            found = mm_nt(picks[duo, rows, :], gmat[2 * SIDE : 4 * SIDE, :])
            hi, lo = halves(found[:, :SIDE] + found[:, SIDE:])
            m2h[level, rows, where_to] = hi
            m2l[level, rows, where_to] = lo
        return carry

    lax.fori_loop(0, levels * (owners // 2), build, 0)

    times = jnp.zeros((nodes, SIDE), F32)
    for i in range(owners):
        wanted = jnp.where(topo_lane, tables[i, levels - 1, 0:1, SIDE:], -1.0)
        times += jnp.where(numbers[0:nodes, :] == wanted, 1.0, 0.0)
    mult[...] = jnp.broadcast_to(jnp.sum(times, axis=1, keepdims=True), (nodes, SIDE))

    def over_states(x):
        total = x[:, :SIDE]
        for k in range(1, states):
            total = total + x[:, k * SIDE : (k + 1) * SIDE]
        return total

    def advance(level, slot, first, last, fresh):
        inner = slice(first, last)
        for r in range(2):
            rows = slice(r * nodes, (r + 1) * nodes)
            bh = m2h[level, rows, inner]
            flat = mm(bh, sums[slot, inner, :])
            flat = flat[:, :SIDE] + flat[:, SIDE:]
            flat = flat + mm(m2l[level, rows, inner], sums[slot, inner, :SIDE])
            flat = jnp.concatenate([flat, flat], axis=1)
            for n in range(states // 2):
                cols = slice(n * ROW, (n + 1) * ROW)
                full = mm(m1h[level, rows, inner], ch[slot, inner, cols])
                full = full + mm(m1h[level, rows, inner], cl[slot, inner, cols])
                full = full + mm(m1l[level, rows, inner], ch[slot, inner, cols])
                full = full + flat
                if not fresh:
                    full = full + pair[rows, cols]
                pair[rows, cols] = full

    own_leaf.wait()
    half = owners // 2
    for part in range(2):
        for i in range(part * half, (part + 1) * half):
            if i:
                leaf_copies[i - 1].wait_recv()
            block = inbox[i]
            rows = slice(i * node_dev, (i + 1) * node_dev)
            total = None
            for k in range(states):
                x = block[:, k, :]
                total = x if k == 0 else total + x
                cols = slice(k * SIDE, (k + 1) * SIDE)
                ch[0, rows, cols], cl[0, rows, cols] = halves(x)
            sums[0, rows, :SIDE], sums[0, rows, SIDE:] = halves(total)
        advance(0, 0, part * half * node_dev, (part + 1) * half * node_dev, part == 0)

    def multiply(slot):
        def body(step, carry):
            rows = pl.ds(pl.multiple_of(step * SIDE, SIDE), SIDE)
            other = pl.ds(pl.multiple_of(nodes + step * SIDE, SIDE), SIDE)
            x = pair[rows, :] * pair[other, :]
            ch[slot, rows, :], cl[slot, rows, :] = halves(x)
            sums[slot, rows, :SIDE], sums[slot, rows, SIDE:] = halves(over_states(x))
            return carry

        lax.fori_loop(0, nodes // SIDE, body, 0)

    slot = 0
    for level in range(1, levels):
        slot = level % 2
        multiply(slot)
        advance(level, slot, 0, nodes, True)

    site_row = lax.broadcasted_iota(jnp.int32, counts.shape, 0)
    count = jnp.sum(
        jnp.where(site_row == me, counts[...].astype(F32) / sites_all, 0.0), axis=0, keepdims=True
    )
    picked = [jnp.zeros((1, SIDE), F32)] * owners
    for first in range(0, nodes, SIDE):
        rows = slice(first, first + SIDE)
        p0 = pair[rows, :]
        p1 = pair[nodes + first : nodes + first + SIDE, :]
        lik = 0.25 * over_states(p0 * p1)
        score = jnp.sum(count * jnp.log(lik), axis=1, keepdims=True)
        here = numbers[rows, :]
        for i in range(owners):
            wanted = jnp.where(topo_lane, tables[i, levels - 1, 0:1, SIDE:], -1.0)
            picked[i] = picked[i] + jnp.sum(
                jnp.where(here == wanted, score, 0.0), axis=0, keepdims=True
            )
        factor = count * 0.25 / lik * mult[rows, :]
        wide = jnp.concatenate([factor] * states, axis=1)
        for r in range(2):
            adj = (p0 if r else p1) * wide
            to = slice(r * nodes + first, r * nodes + first + SIDE)
            ahi[to, :], alo[to, :] = halves(adj)
            adj_sums[to, :SIDE], adj_sums[to, SIDE:] = halves(over_states(adj))

    def products(step, carry):
        cols = pl.ds(pl.multiple_of(step * ROW, ROW), ROW)
        ah, al = ahi[cols, :], alo[cols, :]
        both = adj_sums[cols, :]
        d1 = mm_nt(ch[slot], ah) + mm_nt(ch[slot], al) + mm_nt(cl[slot], ah)
        turned = jnp.concatenate([both[:, SIDE:], both[:, :SIDE]], axis=1)
        d2 = mm_nt(sums[slot], both) + mm_nt(sums[slot], turned)
        d1h, d1l = halves(d1)
        d2h, d2l = halves(d2)
        for i in range(owners):
            rows = slice(i * node_dev, (i + 1) * node_dev)
            for n, piece in enumerate((d1h, d1l, d2h, d2l)):
                dst[i, n * node_dev : (n + 1) * node_dev, cols] = piece[rows, :]
        return carry

    lax.fori_loop(0, 2 * nodes // ROW, products, 0)

    edge_iota = lax.broadcasted_iota(jnp.int32, (node_dev, ROW), 0).astype(F32)
    last = levels - 1
    first_copies = []
    for step in range(owners):
        i = (step + 1) % owners
        found = mm(dst[i], picks[i // 2, :, (i % 2) * ROW : (i % 2 + 1) * ROW])
        hot = edge_iota == tables[i, last, 0:1, :]
        d1 = found[:node_dev] + found[node_dev : 2 * node_dev]
        d2 = found[2 * node_dev : 3 * node_dev] + found[3 * node_dev :]
        q = tables[i, last, 3:4, :]
        mixed = jnp.where(hot, q * d1 + (1.0 - q) * 0.25 * d2, 0.0)
        grads = jnp.sum(mixed, axis=0, keepdims=True)
        grads = grads + jnp.concatenate([jnp.zeros((1, SIDE), F32), picked[i]], axis=1)
        send1[i] = jnp.broadcast_to(grads, (8, ROW))
        if i == 0:
            continue
        copy = pltpu.make_async_remote_copy(
            src_ref=send1.at[i],
            dst_ref=recv1.at[i],
            send_sem=r1_send.at[i],
            recv_sem=r1_recv.at[i],
            device_id={"node": lax.rem(me - i + owners, owners)},
            device_id_type=MESH,
        )
        copy.start()
        first_copies.append(copy)
    total = send1[0]
    for i in range(1, owners):
        first_copies[i - 1].wait_recv()
        total = total + recv1[i]
    send2[...] = total
    recv2[my_site] = total
    second_copies = []
    for i in range(1, site_ways):
        copy = pltpu.make_async_remote_copy(
            src_ref=send2,
            dst_ref=recv2.at[my_site],
            send_sem=r2_send.at[i],
            recv_sem=r2_recv.at[i],
            device_id={"site": lax.rem(my_site + i, site_ways)},
            device_id_type=MESH,
        )
        copy.start()
        second_copies.append(copy)
    for copy in meta_copies + leaf_copies + first_copies:
        copy.wait_send()
    for copy in second_copies:
        copy.wait_recv()
    total = recv2[0]
    for i in range(1, site_ways):
        total = total + recv2[i]
    grad_out[...] = total[0, 0:edge_dev]
    tail = total[0:1, SIDE:]
    which = (lane - SIDE // 2) // topo_shape[1]
    here = jnp.zeros((1, SIDE), F32)
    for t in range(topo_shape[0]):
        mine = topo_lane & (which == t)
        score = jnp.sum(jnp.where(mine, tail, 0.0), axis=1, keepdims=True)
        here = here + jnp.where(lane == t, score, 0.0)
    loglik_out[...] = here[0, 0 : topo_shape[0]]
    for copy in second_copies:
        copy.wait_send()


def by_sites(leaf_partials, dag_edges, weights, lengths, counts, topo_nodes):
    node_dev, states, site_dev = leaf_partials.shape
    levels, edge_dev, _ = dag_edges.shape
    owners, site_ways = lax.axis_size("node"), lax.axis_size("site")
    nodes = owners * node_dev
    wide = states * SIDE
    far = pl.BlockSpec(memory_space=pltpu.HBM)
    near = pl.BlockSpec(memory_space=pltpu.VMEM)
    operator = pltpu.VMEM((levels, 2 * nodes, nodes), BF16)
    loglik, grads = pl.pallas_call(
        functools.partial(
            kernel,
            (
                owners,
                site_ways,
                node_dev,
                states,
                levels,
                topo_nodes.shape,
                site_dev * site_ways,
            ),
        ),
        out_shape=(
            jax.ShapeDtypeStruct((topo_nodes.shape[0],), F32),
            jax.ShapeDtypeStruct((edge_dev,), F32),
        ),
        in_specs=[far] * 6,
        out_specs=(near, near),
        scratch_shapes=[
            pltpu.VMEM((levels, 3, edge_dev), jnp.int32),
            pltpu.VMEM((levels, edge_dev), F32),
            pltpu.VMEM((levels, edge_dev), F32),
            pltpu.VMEM((owners, SIDE), jnp.int32),
            pltpu.VMEM(topo_nodes.shape, jnp.int32),
            pltpu.VMEM((levels, 4, ROW), F32),
            pltpu.VMEM((owners, node_dev, states, SIDE), F32),
            pltpu.VMEM((owners, levels, 4, ROW), F32),
            operator,
            operator,
            operator,
            operator,
            pltpu.VMEM((owners // 2, 2 * nodes, 2 * ROW), BF16),
            pltpu.VMEM((4 * SIDE, 2 * ROW), BF16),
            pltpu.VMEM((2, nodes, wide), BF16),
            pltpu.VMEM((2, nodes, wide), BF16),
            pltpu.VMEM((2, nodes, 2 * SIDE), BF16),
            pltpu.VMEM((2 * nodes, wide), F32),
            pltpu.VMEM((nodes, SIDE), F32),
            pltpu.VMEM((2 * nodes, wide), BF16),
            pltpu.VMEM((2 * nodes, wide), BF16),
            pltpu.VMEM((2 * nodes, 2 * SIDE), BF16),
            pltpu.VMEM((owners, 4 * node_dev, 2 * nodes), BF16),
            pltpu.VMEM((2 * nodes, SIDE), F32),
            pltpu.VMEM((nodes, SIDE), F32),
            pltpu.VMEM((owners, 8, ROW), F32),
            pltpu.VMEM((owners, 8, ROW), F32),
            pltpu.VMEM((8, ROW), F32),
            pltpu.VMEM((site_ways, 8, ROW), F32),
            pltpu.SemaphoreType.DMA((owners,)),
            pltpu.SemaphoreType.DMA((owners,)),
            pltpu.SemaphoreType.DMA((owners,)),
            pltpu.SemaphoreType.DMA((owners,)),
            pltpu.SemaphoreType.DMA((6,)),
            pltpu.SemaphoreType.DMA((owners,)),
            pltpu.SemaphoreType.DMA((owners,)),
            pltpu.SemaphoreType.DMA((site_ways,)),
            pltpu.SemaphoreType.DMA((site_ways,)),
        ],
        compiler_params=pltpu.CompilerParams(
            collective_id=0, has_side_effects=True, vmem_limit_bytes=64 * 2**20
        ),
    )(
        leaf_partials,
        jnp.transpose(dag_edges, (0, 2, 1)),
        weights,
        lengths,
        counts.reshape(owners, SIDE),
        topo_nodes,
    )
    return loglik, grads


def either(leaf_partials, dag_edges, weights, lengths, counts, topo_nodes):
    node_dev, states, site_dev = leaf_partials.shape
    owners = lax.axis_size("node")
    fits = (
        site_dev == owners * SIDE
        and 2 * node_dev == SIDE
        and owners % 2 == 0
        and owners <= 8
        and dag_edges.shape[1] == ROW * 3 // 4
        and topo_nodes.size <= ROW // 4
    )
    form = by_sites if fits else on_device
    return form(leaf_partials, dag_edges, weights, lengths, counts, topo_nodes)


def solution(mesh):
    return jax.shard_map(
        either,
        mesh=mesh,
        in_specs=(
            P("node", None, "site"),
            P(None, "node", None),
            P(None, "node"),
            P(None, "node"),
            P("site"),
            P("node", None),
        ),
        out_specs=(P("node"), P("node")),
        check_vma=False,
    )
```

```python
import functools

import jax
import jax.numpy as jnp
from jax import lax
from jax.experimental import pallas as pl
from jax.experimental.pallas import tpu as pltpu
from jax.sharding import PartitionSpec as P


def transit(child_rows, branch):
    survival = jnp.exp(branch * (-4.0 / 3.0))[:, None, None]
    return survival * child_rows + (1.0 - survival) * 0.25 * jnp.sum(
        child_rows, axis=1, keepdims=True
    )


def on_device(leaf_partials, dag_edges, weights, lengths, counts, topo_nodes):
    node_dev, states, site_dev = leaf_partials.shape
    level_count, edge_dev = (dag_edges.shape[0], dag_edges.shape[1])
    owners = lax.axis_size("node")
    device = lax.axis_index("node")
    nodes_all = node_dev * owners
    sites_all = site_dev * lax.axis_size("site")
    scaled = counts.astype(jnp.float32) / sites_all
    incidence = lax.all_gather(topo_nodes, "node", axis=0, tiled=True)
    multiplicity = jax.ops.segment_sum(
        jnp.ones((incidence.size,), jnp.float32), incidence.reshape(-1), num_segments=nodes_all
    )
    capacity = 4 * node_dev // owners
    slots_all = owners * capacity
    current = leaf_partials
    for level_index in range(level_count):
        child_index = dag_edges[level_index, :, 0] - device * node_dev
        parents = dag_edges[level_index, :, 1]
        rotation = dag_edges[level_index, :, 2]
        message = transit(current[child_index], lengths[level_index])
        owner_dev = parents // node_dev
        one_hot = (owner_dev[:, None] == jnp.arange(owners)[None, :]).astype(jnp.int32)
        slot_rank = jnp.sum((jnp.cumsum(one_hot, axis=0) - one_hot) * one_hot, axis=1)
        slot_index = owner_dev * capacity + slot_rank
        pair_code = ((parents - owner_dev * node_dev) * 2 + rotation).astype(jnp.float32)
        buffer = jnp.zeros((slots_all, states, site_dev), jnp.float32).at[slot_index].set(message)
        code_buffer = jnp.full((slots_all,), -1.0, jnp.float32).at[slot_index].set(pair_code)
        weight_buffer = (
            jnp.zeros((slots_all,), jnp.float32).at[slot_index].set(weights[level_index])
        )
        received, received_codes, received_weights = (
            lax.all_to_all(
                buffer.reshape(owners, capacity, states, site_dev),
                "node",
                split_axis=0,
                concat_axis=0,
                tiled=True,
            ),
            lax.all_to_all(
                code_buffer.reshape(owners, capacity),
                "node",
                split_axis=0,
                concat_axis=0,
                tiled=True,
            ),
            lax.all_to_all(
                weight_buffer.reshape(owners, capacity),
                "node",
                split_axis=0,
                concat_axis=0,
                tiled=True,
            ),
        )
        flat_rows = received.reshape(slots_all, states * site_dev)
        selector = (
            received_codes.reshape(-1).astype(jnp.int32)[None, :]
            == jnp.arange(2 * node_dev)[:, None]
        ).astype(jnp.float32)
        summed = jnp.dot(
            selector * received_weights.reshape(-1)[None, :],
            flat_rows,
            precision=lax.Precision.HIGHEST,
            preferred_element_type=jnp.float32,
        )
        pair_sums = summed.reshape(node_dev, 2, states, site_dev)
        current = pair_sums[:, 0] * pair_sums[:, 1]
    denominator = 0.25 * jnp.sum(current, axis=1)
    node_part = jnp.sum(scaled[None, :] * jnp.log(denominator), axis=1)
    adjoint = pair_sums[:, ::-1] * (scaled[None, :] * 0.25 / denominator)[:, None, None, :]
    adjoint_slots = jnp.dot(
        selector.T,
        adjoint.reshape(2 * node_dev, states * site_dev),
        precision=lax.Precision.HIGHEST,
        preferred_element_type=jnp.float32,
    )
    grad_part = jnp.sum(flat_rows * adjoint_slots, axis=1)
    node_scores, slot_grads = lax.psum((node_part, grad_part), "site")
    own_mult = lax.dynamic_slice_in_dim(multiplicity, device * node_dev, node_dev)
    pair_mult = jnp.repeat(own_mult, 2)
    slot_mult = jnp.dot(
        selector.T, pair_mult, precision=lax.Precision.HIGHEST, preferred_element_type=jnp.float32
    )
    returned = lax.all_to_all(
        (slot_grads * slot_mult).reshape(owners, capacity),
        "node",
        split_axis=0,
        concat_axis=0,
        tiled=True,
    )
    edge_gradient = returned.reshape(-1)[slot_index]
    score_table = lax.all_gather(node_scores, "node", axis=0, tiled=True)
    topology_loglik = jnp.sum(score_table[topo_nodes], axis=1)
    return (topology_loglik, edge_gradient)


MESH = pl.DeviceIdType.MESH
F32 = jnp.float32
BF16 = jnp.bfloat16
ROW = 256
SIDE = 128


def halves(x):
    hi = x.astype(BF16)
    return hi, (x - hi.astype(F32)).astype(BF16)


def mm(a, b):
    return jnp.dot(a, b, preferred_element_type=F32)


def mm_nt(a, b):
    return lax.dot_general(a, b, (((1,), (1,)), ((), ())), preferred_element_type=F32)


def kernel(
    dims,
    leaf,
    edges_hbm,
    weights_hbm,
    lengths_hbm,
    counts_hbm,
    topo_hbm,
    loglik_out,
    grad_out,
    edges,
    weights,
    lengths,
    counts,
    topo,
    meta,
    inbox,
    tables,
    m1,
    m2h,
    m2l,
    picks,
    gmat,
    stack,
    sums,
    pair,
    dst,
    numbers,
    mult,
    send1,
    recv1,
    send2,
    recv2,
    leaf_send,
    leaf_recv,
    meta_send,
    meta_recv,
    own_sem,
    r1_send,
    r1_recv,
    r2_send,
    r2_recv,
):
    owners, site_ways, node_dev, states, levels, topo_shape, sites_all = dims
    nodes = owners * node_dev
    edge_dev = edges.shape[2]
    topo_here = topo_shape[0] * topo_shape[1]
    me = lax.axis_index("node")
    my_site = lax.axis_index("site")

    small = []
    for n, (a, b) in enumerate(
        (
            (edges_hbm, edges),
            (weights_hbm, weights),
            (lengths_hbm, lengths),
            (counts_hbm, counts),
            (topo_hbm, topo),
        )
    ):
        copy = pltpu.make_async_copy(a, b, own_sem.at[n])
        copy.start()
        small.append(copy)
    own_leaf = pltpu.make_async_copy(
        leaf.at[:, :, pl.ds(pl.multiple_of(me * SIDE, SIDE), SIDE)], inbox.at[0], own_sem.at[5]
    )
    own_leaf.start()

    barrier = pltpu.get_barrier_semaphore()
    for i in range(1, owners):
        pl.semaphore_signal(
            barrier, inc=1, device_id={"node": lax.rem(me + i, owners)}, device_id_type=MESH
        )
    for i in range(1, site_ways):
        pl.semaphore_signal(
            barrier, inc=1, device_id={"site": lax.rem(my_site + i, site_ways)}, device_id_type=MESH
        )

    meta[...] = jnp.full(meta.shape, -1.0, F32)
    for copy in small:
        copy.wait()
    for level in range(levels):
        child = edges[level, 0:1, :] - me * node_dev
        code = edges[level, 2:3, :] * nodes + edges[level, 1:2, :]
        meta[level, 0:1, 0:edge_dev] = child.astype(F32)
        meta[level, 1:2, 0:edge_dev] = code.astype(F32)
        meta[level, 2:3, 0:edge_dev] = weights[level : level + 1, :]
        meta[level, 3:4, 0:edge_dev] = jnp.exp(lengths[level : level + 1, :] * (-4.0 / 3.0))
    for t in range(topo_shape[0]):
        first = edge_dev + t * topo_shape[1]
        meta[levels - 1, 0:1, first : first + topo_shape[1]] = topo[t : t + 1, :].astype(F32)

    pl.semaphore_wait(barrier, owners - 1 + site_ways - 1)

    meta_copies, leaf_copies = [], []
    for i in range(1, owners):
        copy = pltpu.make_async_remote_copy(
            src_ref=meta,
            dst_ref=tables.at[i],
            send_sem=meta_send.at[i],
            recv_sem=meta_recv.at[i],
            device_id={"node": lax.rem(me + i, owners)},
            device_id_type=MESH,
        )
        copy.start()
        meta_copies.append(copy)
    for i in range(1, owners):
        target = lax.rem(me + i, owners)
        copy = pltpu.make_async_remote_copy(
            src_ref=leaf.at[:, :, pl.ds(pl.multiple_of(target * SIDE, SIDE), SIDE)],
            dst_ref=inbox.at[i],
            send_sem=leaf_send.at[i],
            recv_sem=leaf_recv.at[i],
            device_id={"node": target},
            device_id_type=MESH,
        )
        copy.start()
        leaf_copies.append(copy)
    tables[0] = meta[...]

    local = lax.broadcasted_iota(jnp.int32, (node_dev, SIDE), 0)
    for r in range(2):
        for i in range(owners):
            first = r * nodes + i * node_dev
            owner = lax.rem(me - i + owners, owners)
            numbers[first : first + node_dev, :] = (
                local + (r * nodes + owner * node_dev)
            ).astype(F32)

    lane = lax.broadcasted_iota(jnp.int32, (1, SIDE), 1)
    topo_lane = (lane >= SIDE // 2) & (lane < SIDE // 2 + topo_here)
    child_iota = lax.broadcasted_iota(jnp.int32, (2 * node_dev, ROW), 0).astype(F32)

    for copy in meta_copies:
        copy.wait_recv()

    half = nodes // 2

    def build(step, carry):
        level = step // (owners // 2)
        duo = lax.rem(step, owners // 2)
        codes = []
        for a in range(2):
            child = tables[2 * duo + a, level, 0:1, :]
            codes.append(tables[2 * duo + a, level, 1:2, :])
            weight = tables[2 * duo + a, level, 2:3, :]
            q = tables[2 * duo + a, level, 3:4, :]
            hot = child_iota == child + float(a * node_dev)
            g1h, g1l = halves(jnp.where(hot, weight * q, 0.0))
            g2h, g2l = halves(jnp.where(hot, weight * (1.0 - q) * 0.25, 0.0))
            columns = slice(a * ROW, (a + 1) * ROW)
            for n, piece in enumerate((g1h, g1l, g2h, g2l)):
                gmat[n * SIDE : (n + 1) * SIDE, columns] = piece
        code = jnp.concatenate(codes, axis=1)

        def choose(part, inner):
            rows = pl.ds(pl.multiple_of(part * SIDE, SIDE), SIDE)
            wide = jnp.concatenate([numbers[rows, :]] * 4, axis=1)
            picks[duo, rows, :] = jnp.where(wide == code, 1.0, 0.0).astype(BF16)
            return inner

        lax.fori_loop(0, 2 * nodes // SIDE, choose, 0)
        where_to = pl.ds(pl.multiple_of(duo * SIDE, SIDE), SIDE)
        base = (duo // (owners // 4)) * 3 * half + lax.rem(duo, owners // 4) * SIDE
        thirds = [pl.ds(pl.multiple_of(base + n * half, SIDE), SIDE) for n in range(3)]
        for r in range(2):
            rows = slice(r * nodes, (r + 1) * nodes)
            found = mm_nt(picks[duo, rows, :], gmat[0 : 2 * SIDE, :])
            hi, lo = halves(found[:, :SIDE] + found[:, SIDE:])
            m1[level, r, :, thirds[0]] = hi
            m1[level, r, :, thirds[1]] = hi
            m1[level, r, :, thirds[2]] = lo
            found = mm_nt(picks[duo, rows, :], gmat[2 * SIDE : 4 * SIDE, :])
            hi, lo = halves(found[:, :SIDE] + found[:, SIDE:])
            m2h[level, r, :, where_to] = hi
            m2l[level, r, :, where_to] = lo
        return carry

    lax.fori_loop(0, levels * (owners // 2), build, 0)

    times = jnp.zeros((nodes, SIDE), F32)
    for i in range(owners):
        wanted = jnp.where(topo_lane, tables[i, levels - 1, 0:1, SIDE:], -1.0)
        times += jnp.where(numbers[0:nodes, :] == wanted, 1.0, 0.0)
    mult[...] = jnp.broadcast_to(jnp.sum(times, axis=1, keepdims=True), (nodes, SIDE))

    def over_states(x):
        total = x[:, :SIDE]
        for k in range(1, states):
            total = total + x[:, k * SIDE : (k + 1) * SIDE]
        return total

    def keep(slot, g, cols, x):
        base = g * 3 * half
        hi, lo = halves(x)
        for n, piece in enumerate((hi, lo, hi)):
            rows = pl.ds(pl.multiple_of(base + n * half, half), half)
            stack[slot, rows, cols] = piece

    def advance(level, slot, parts, fresh, store, later):
        inner = slice(parts[0] * half, parts[1] * half)
        long = slice(parts[0] * 3 * half, parts[1] * 3 * half)

        def body(g, carry):
            rows = pl.ds(pl.multiple_of(g * half, half), half)
            high = m2h[level, :, rows, inner].reshape(2 * half, -1)
            low = m2l[level, :, rows, inner].reshape(2 * half, -1)
            flat = mm(high, sums[slot, inner, :])
            flat = flat[:, :SIDE] + flat[:, SIDE:] + mm(low, sums[slot, inner, :SIDE])
            flat = jnp.concatenate([flat, flat], axis=1)
            left = m1[level, :, rows, long].reshape(2 * half, -1)
            total = None
            for n in range(states // 2):
                cols = slice(n * ROW, (n + 1) * ROW)
                full = mm(left, stack[slot, long, cols]) + flat
                if not fresh:
                    full = full + pair[:, rows, cols].reshape(2 * half, ROW)
                if store:
                    pair[:, rows, cols] = full.reshape(2, half, ROW)
                if later is not None:
                    x = full[:half] * full[half:]
                    keep(later, g, cols, x)
                    x = x[:, :SIDE] + x[:, SIDE:]
                    total = x if n == 0 else total + x
            if later is not None:
                sums[later, rows, :SIDE], sums[later, rows, SIDE:] = halves(total)
            return carry

        lax.fori_loop(0, 2, body, 0)

    own_leaf.wait()
    for part in range(2):
        for i in range(part * owners // 2, (part + 1) * owners // 2):
            if i:
                leaf_copies[i - 1].wait_recv()
            block = inbox[i]
            rows = slice(i * node_dev, (i + 1) * node_dev)
            base = part * 3 * half + i * node_dev - part * half
            total = None
            for k in range(states):
                x = block[:, k, :]
                total = x if k == 0 else total + x
                hi, lo = halves(x)
                for n, piece in enumerate((hi, lo, hi)):
                    to = slice(base + n * half, base + n * half + node_dev)
                    stack[0, to, k * SIDE : (k + 1) * SIDE] = piece
            sums[0, rows, :SIDE], sums[0, rows, SIDE:] = halves(total)
        advance(0, 0, (part, part + 1), part == 0, part == 0, 1 if part else None)
    for level in range(1, levels):
        last_one = level == levels - 1
        advance(level, level % 2, (0, 2), True, last_one, None if last_one else (level + 1) % 2)
    slot = (levels - 1) % 2

    site_row = lax.broadcasted_iota(jnp.int32, counts.shape, 0)
    count = jnp.sum(
        jnp.where(site_row == me, counts[...].astype(F32) / sites_all, 0.0), axis=0, keepdims=True
    )

    def products(step, picked):
        rows = pl.ds(pl.multiple_of(step * SIDE, SIDE), SIDE)
        p0 = pair[0, rows, :]
        p1 = pair[1, rows, :]
        lik = 0.25 * over_states(p0 * p1)
        factor = count * 0.25 / lik * mult[rows, :]
        wide = jnp.concatenate([factor] * states, axis=1)
        adj = jnp.concatenate([p1 * wide, p0 * wide], axis=0)
        ah, al = halves(adj)
        sh, sl = halves(over_states(adj))
        both = jnp.concatenate([sh, sl], axis=1)
        turned = jnp.concatenate([sl, sh], axis=1)
        for part in range(2):
            base = part * 3 * half
            d1 = mm_nt(stack[slot, base : base + 2 * half, :], ah)
            d1 = d1[:half] + d1[half:] + mm_nt(stack[slot, base : base + half, :], al)
            own = sums[slot, part * half : (part + 1) * half, :]
            d2 = mm_nt(own, both) + mm_nt(own, turned)
            pieces = halves(d1) + halves(d2)
            for i in range(owners // 2):
                inner = slice(i * node_dev, (i + 1) * node_dev)
                for n, piece in enumerate(pieces):
                    to = slice(n * node_dev, (n + 1) * node_dev)
                    for r in range(2):
                        cols = pl.ds(pl.multiple_of(r * nodes + step * SIDE, SIDE), SIDE)
                        dst[part * owners // 2 + i, to, cols] = piece[
                            inner, r * SIDE : (r + 1) * SIDE
                        ]
        score = jnp.sum(count * jnp.log(lik), axis=1, keepdims=True)
        here = numbers[rows, :]
        found = []
        for i in range(owners):
            wanted = jnp.where(topo_lane, tables[i, levels - 1, 0:1, SIDE:], -1.0)
            found.append(
                picked[i]
                + jnp.sum(jnp.where(here == wanted, score, 0.0), axis=0, keepdims=True)
            )
        return tuple(found)

    picked = lax.fori_loop(
        0, nodes // SIDE, products, tuple(jnp.zeros((1, SIDE), F32) for _ in range(owners))
    )

    edge_iota = lax.broadcasted_iota(jnp.int32, (node_dev, ROW), 0).astype(F32)
    last = levels - 1
    first_copies = []
    for step in range(owners):
        i = (step + 1) % owners
        found = mm(dst[i], picks[i // 2, :, (i % 2) * ROW : (i % 2 + 1) * ROW])
        hot = edge_iota == tables[i, last, 0:1, :]
        d1 = found[:node_dev] + found[node_dev : 2 * node_dev]
        d2 = found[2 * node_dev : 3 * node_dev] + found[3 * node_dev :]
        q = tables[i, last, 3:4, :]
        mixed = jnp.where(hot, q * d1 + (1.0 - q) * 0.25 * d2, 0.0)
        grads = jnp.sum(mixed, axis=0, keepdims=True)
        grads = grads + jnp.concatenate([jnp.zeros((1, SIDE), F32), picked[i]], axis=1)
        send1[i] = jnp.broadcast_to(grads, (8, ROW))
        if i == 0:
            continue
        copy = pltpu.make_async_remote_copy(
            src_ref=send1.at[i],
            dst_ref=recv1.at[i],
            send_sem=r1_send.at[i],
            recv_sem=r1_recv.at[i],
            device_id={"node": lax.rem(me - i + owners, owners)},
            device_id_type=MESH,
        )
        copy.start()
        first_copies.append(copy)
    total = send1[0]
    for i in range(1, owners):
        first_copies[i - 1].wait_recv()
        total = total + recv1[i]
    send2[...] = total
    recv2[my_site] = total
    second_copies = []
    for i in range(1, site_ways):
        copy = pltpu.make_async_remote_copy(
            src_ref=send2,
            dst_ref=recv2.at[my_site],
            send_sem=r2_send.at[i],
            recv_sem=r2_recv.at[i],
            device_id={"site": lax.rem(my_site + i, site_ways)},
            device_id_type=MESH,
        )
        copy.start()
        second_copies.append(copy)
    for copy in meta_copies + leaf_copies + first_copies:
        copy.wait_send()
    for copy in second_copies:
        copy.wait_recv()
    total = recv2[0]
    for i in range(1, site_ways):
        total = total + recv2[i]
    grad_out[...] = total[0, 0:edge_dev]
    tail = total[0:1, SIDE:]
    which = (lane - SIDE // 2) // topo_shape[1]
    here = jnp.zeros((1, SIDE), F32)
    for t in range(topo_shape[0]):
        mine = topo_lane & (which == t)
        score = jnp.sum(jnp.where(mine, tail, 0.0), axis=1, keepdims=True)
        here = here + jnp.where(lane == t, score, 0.0)
    loglik_out[...] = here[0, 0 : topo_shape[0]]
    for copy in second_copies:
        copy.wait_send()


def by_sites(leaf_partials, dag_edges, weights, lengths, counts, topo_nodes):
    node_dev, states, site_dev = leaf_partials.shape
    levels, edge_dev, _ = dag_edges.shape
    owners, site_ways = lax.axis_size("node"), lax.axis_size("site")
    nodes = owners * node_dev
    wide = states * SIDE
    far = pl.BlockSpec(memory_space=pltpu.HBM)
    near = pl.BlockSpec(memory_space=pltpu.VMEM)
    operator = pltpu.VMEM((levels, 2, nodes, nodes), BF16)
    loglik, grads = pl.pallas_call(
        functools.partial(
            kernel,
            (
                owners,
                site_ways,
                node_dev,
                states,
                levels,
                topo_nodes.shape,
                site_dev * site_ways,
            ),
        ),
        out_shape=(
            jax.ShapeDtypeStruct((topo_nodes.shape[0],), F32),
            jax.ShapeDtypeStruct((edge_dev,), F32),
        ),
        in_specs=[far] * 6,
        out_specs=(near, near),
        scratch_shapes=[
            pltpu.VMEM((levels, 3, edge_dev), jnp.int32),
            pltpu.VMEM((levels, edge_dev), F32),
            pltpu.VMEM((levels, edge_dev), F32),
            pltpu.VMEM((owners, SIDE), jnp.int32),
            pltpu.VMEM(topo_nodes.shape, jnp.int32),
            pltpu.VMEM((levels, 4, ROW), F32),
            pltpu.VMEM((owners, node_dev, states, SIDE), F32),
            pltpu.VMEM((owners, levels, 4, ROW), F32),
            pltpu.VMEM((levels, 2, nodes, 3 * nodes), BF16),
            operator,
            operator,
            pltpu.VMEM((owners // 2, 2 * nodes, 2 * ROW), BF16),
            pltpu.VMEM((4 * SIDE, 2 * ROW), BF16),
            pltpu.VMEM((2, 3 * nodes, wide), BF16),
            pltpu.VMEM((2, nodes, 2 * SIDE), BF16),
            pltpu.VMEM((2, nodes, wide), F32),
            pltpu.VMEM((owners, 4 * node_dev, 2 * nodes), BF16),
            pltpu.VMEM((2 * nodes, SIDE), F32),
            pltpu.VMEM((nodes, SIDE), F32),
            pltpu.VMEM((owners, 8, ROW), F32),
            pltpu.VMEM((owners, 8, ROW), F32),
            pltpu.VMEM((8, ROW), F32),
            pltpu.VMEM((site_ways, 8, ROW), F32),
            pltpu.SemaphoreType.DMA((owners,)),
            pltpu.SemaphoreType.DMA((owners,)),
            pltpu.SemaphoreType.DMA((owners,)),
            pltpu.SemaphoreType.DMA((owners,)),
            pltpu.SemaphoreType.DMA((6,)),
            pltpu.SemaphoreType.DMA((owners,)),
            pltpu.SemaphoreType.DMA((owners,)),
            pltpu.SemaphoreType.DMA((site_ways,)),
            pltpu.SemaphoreType.DMA((site_ways,)),
        ],
        compiler_params=pltpu.CompilerParams(
            collective_id=0, has_side_effects=True, vmem_limit_bytes=64 * 2**20
        ),
    )(
        leaf_partials,
        jnp.transpose(dag_edges, (0, 2, 1)),
        weights,
        lengths,
        counts.reshape(owners, SIDE),
        topo_nodes,
    )
    return loglik, grads


def either(leaf_partials, dag_edges, weights, lengths, counts, topo_nodes):
    node_dev, states, site_dev = leaf_partials.shape
    owners = lax.axis_size("node")
    fits = (
        site_dev == owners * SIDE
        and 2 * node_dev == SIDE
        and owners % 4 == 0
        and owners <= 8
        and dag_edges.shape[1] == ROW * 3 // 4
        and topo_nodes.size <= ROW // 4
    )
    form = by_sites if fits else on_device
    return form(leaf_partials, dag_edges, weights, lengths, counts, topo_nodes)


def solution(mesh):
    return jax.shard_map(
        either,
        mesh=mesh,
        in_specs=(
            P("node", None, "site"),
            P(None, "node", None),
            P(None, "node"),
            P(None, "node"),
            P("site"),
            P("node", None),
        ),
        out_specs=(P("node"), P("node")),
        check_vma=False,
    )
```

```python
import functools

import jax
import jax.numpy as jnp
from jax import lax
from jax.experimental import pallas as pl
from jax.experimental.pallas import tpu as pltpu
from jax.sharding import PartitionSpec as P


def transit(child_rows, branch):
    survival = jnp.exp(branch * (-4.0 / 3.0))[:, None, None]
    return survival * child_rows + (1.0 - survival) * 0.25 * jnp.sum(
        child_rows, axis=1, keepdims=True
    )


def on_device(leaf_partials, dag_edges, weights, lengths, counts, topo_nodes):
    node_dev, states, site_dev = leaf_partials.shape
    level_count, edge_dev = (dag_edges.shape[0], dag_edges.shape[1])
    owners = lax.axis_size("node")
    device = lax.axis_index("node")
    nodes_all = node_dev * owners
    sites_all = site_dev * lax.axis_size("site")
    scaled = counts.astype(jnp.float32) / sites_all
    incidence = lax.all_gather(topo_nodes, "node", axis=0, tiled=True)
    multiplicity = jax.ops.segment_sum(
        jnp.ones((incidence.size,), jnp.float32), incidence.reshape(-1), num_segments=nodes_all
    )
    capacity = 4 * node_dev // owners
    slots_all = owners * capacity
    current = leaf_partials
    for level_index in range(level_count):
        child_index = dag_edges[level_index, :, 0] - device * node_dev
        parents = dag_edges[level_index, :, 1]
        rotation = dag_edges[level_index, :, 2]
        message = transit(current[child_index], lengths[level_index])
        owner_dev = parents // node_dev
        one_hot = (owner_dev[:, None] == jnp.arange(owners)[None, :]).astype(jnp.int32)
        slot_rank = jnp.sum((jnp.cumsum(one_hot, axis=0) - one_hot) * one_hot, axis=1)
        slot_index = owner_dev * capacity + slot_rank
        pair_code = ((parents - owner_dev * node_dev) * 2 + rotation).astype(jnp.float32)
        buffer = jnp.zeros((slots_all, states, site_dev), jnp.float32).at[slot_index].set(message)
        code_buffer = jnp.full((slots_all,), -1.0, jnp.float32).at[slot_index].set(pair_code)
        weight_buffer = (
            jnp.zeros((slots_all,), jnp.float32).at[slot_index].set(weights[level_index])
        )
        received, received_codes, received_weights = (
            lax.all_to_all(
                buffer.reshape(owners, capacity, states, site_dev),
                "node",
                split_axis=0,
                concat_axis=0,
                tiled=True,
            ),
            lax.all_to_all(
                code_buffer.reshape(owners, capacity),
                "node",
                split_axis=0,
                concat_axis=0,
                tiled=True,
            ),
            lax.all_to_all(
                weight_buffer.reshape(owners, capacity),
                "node",
                split_axis=0,
                concat_axis=0,
                tiled=True,
            ),
        )
        flat_rows = received.reshape(slots_all, states * site_dev)
        selector = (
            received_codes.reshape(-1).astype(jnp.int32)[None, :]
            == jnp.arange(2 * node_dev)[:, None]
        ).astype(jnp.float32)
        summed = jnp.dot(
            selector * received_weights.reshape(-1)[None, :],
            flat_rows,
            precision=lax.Precision.HIGHEST,
            preferred_element_type=jnp.float32,
        )
        pair_sums = summed.reshape(node_dev, 2, states, site_dev)
        current = pair_sums[:, 0] * pair_sums[:, 1]
    denominator = 0.25 * jnp.sum(current, axis=1)
    node_part = jnp.sum(scaled[None, :] * jnp.log(denominator), axis=1)
    adjoint = pair_sums[:, ::-1] * (scaled[None, :] * 0.25 / denominator)[:, None, None, :]
    adjoint_slots = jnp.dot(
        selector.T,
        adjoint.reshape(2 * node_dev, states * site_dev),
        precision=lax.Precision.HIGHEST,
        preferred_element_type=jnp.float32,
    )
    grad_part = jnp.sum(flat_rows * adjoint_slots, axis=1)
    node_scores, slot_grads = lax.psum((node_part, grad_part), "site")
    own_mult = lax.dynamic_slice_in_dim(multiplicity, device * node_dev, node_dev)
    pair_mult = jnp.repeat(own_mult, 2)
    slot_mult = jnp.dot(
        selector.T, pair_mult, precision=lax.Precision.HIGHEST, preferred_element_type=jnp.float32
    )
    returned = lax.all_to_all(
        (slot_grads * slot_mult).reshape(owners, capacity),
        "node",
        split_axis=0,
        concat_axis=0,
        tiled=True,
    )
    edge_gradient = returned.reshape(-1)[slot_index]
    score_table = lax.all_gather(node_scores, "node", axis=0, tiled=True)
    topology_loglik = jnp.sum(score_table[topo_nodes], axis=1)
    return (topology_loglik, edge_gradient)


MESH = pl.DeviceIdType.MESH
F32 = jnp.float32
BF16 = jnp.bfloat16
ROW = 256
SIDE = 128


def halves(x):
    hi = x.astype(BF16)
    return hi, (x - hi.astype(F32)).astype(BF16)


def mm(a, b):
    return jnp.dot(a, b, preferred_element_type=F32)


def mm_nt(a, b):
    return lax.dot_general(a, b, (((1,), (1,)), ((), ())), preferred_element_type=F32)


def kernel(
    dims,
    leaf,
    edges_hbm,
    weights_hbm,
    lengths_hbm,
    counts_hbm,
    topo_hbm,
    loglik_out,
    grad_out,
    edges,
    weights,
    lengths,
    counts,
    topo,
    meta,
    inbox,
    tables,
    m1h,
    m1l,
    m2h,
    m2l,
    picks,
    gmat,
    ch,
    cl,
    sums,
    pair,
    lik_sum,
    ahi,
    alo,
    adj_sums,
    dst,
    numbers,
    mult,
    send1,
    recv1,
    send2,
    recv2,
    leaf_send,
    leaf_recv,
    meta_send,
    meta_recv,
    own_sem,
    r1_send,
    r1_recv,
    r2_send,
    r2_recv,
):
    owners, site_ways, node_dev, states, levels, topo_shape, sites_all = dims
    nodes = owners * node_dev
    edge_dev = edges.shape[2]
    topo_here = topo_shape[0] * topo_shape[1]
    me = lax.axis_index("node")
    my_site = lax.axis_index("site")

    small = []
    for n, (a, b) in enumerate(
        (
            (edges_hbm, edges),
            (weights_hbm, weights),
            (lengths_hbm, lengths),
            (counts_hbm, counts),
            (topo_hbm, topo),
        )
    ):
        copy = pltpu.make_async_copy(a, b, own_sem.at[n])
        copy.start()
        small.append(copy)
    own_leaf = pltpu.make_async_copy(
        leaf.at[:, :, pl.ds(pl.multiple_of(me * SIDE, SIDE), SIDE)], inbox.at[0], own_sem.at[5]
    )
    own_leaf.start()

    barrier = pltpu.get_barrier_semaphore()
    for i in range(1, owners):
        pl.semaphore_signal(
            barrier, inc=1, device_id={"node": lax.rem(me + i, owners)}, device_id_type=MESH
        )
    for i in range(1, site_ways):
        pl.semaphore_signal(
            barrier, inc=1, device_id={"site": lax.rem(my_site + i, site_ways)}, device_id_type=MESH
        )

    meta[...] = jnp.full(meta.shape, -1.0, F32)
    for copy in small:
        copy.wait()
    for level in range(levels):
        child = edges[level, 0:1, :] - me * node_dev
        code = edges[level, 2:3, :] * nodes + edges[level, 1:2, :]
        meta[level, 0:1, 0:edge_dev] = child.astype(F32)
        meta[level, 1:2, 0:edge_dev] = code.astype(F32)
        meta[level, 2:3, 0:edge_dev] = weights[level : level + 1, :]
        meta[level, 3:4, 0:edge_dev] = jnp.exp(lengths[level : level + 1, :] * (-4.0 / 3.0))
    for t in range(topo_shape[0]):
        first = edge_dev + t * topo_shape[1]
        meta[levels - 1, 0:1, first : first + topo_shape[1]] = topo[t : t + 1, :].astype(F32)

    pl.semaphore_wait(barrier, owners - 1 + site_ways - 1)

    meta_copies, leaf_copies = [], []
    for i in range(1, owners):
        copy = pltpu.make_async_remote_copy(
            src_ref=meta,
            dst_ref=tables.at[i],
            send_sem=meta_send.at[i],
            recv_sem=meta_recv.at[i],
            device_id={"node": lax.rem(me + i, owners)},
            device_id_type=MESH,
        )
        copy.start()
        meta_copies.append(copy)
    for i in range(1, owners):
        target = lax.rem(me + i, owners)
        copy = pltpu.make_async_remote_copy(
            src_ref=leaf.at[:, :, pl.ds(pl.multiple_of(target * SIDE, SIDE), SIDE)],
            dst_ref=inbox.at[i],
            send_sem=leaf_send.at[i],
            recv_sem=leaf_recv.at[i],
            device_id={"node": target},
            device_id_type=MESH,
        )
        copy.start()
        leaf_copies.append(copy)
    tables[0] = meta[...]

    local = lax.broadcasted_iota(jnp.int32, (node_dev, SIDE), 0)
    for r in range(2):
        for i in range(owners):
            first = r * nodes + i * node_dev
            owner = lax.rem(me - i + owners, owners)
            numbers[first : first + node_dev, :] = (
                local + (r * nodes + owner * node_dev)
            ).astype(F32)

    lane = lax.broadcasted_iota(jnp.int32, (1, SIDE), 1)
    topo_lane = (lane >= SIDE // 2) & (lane < SIDE // 2 + topo_here)
    child_iota = lax.broadcasted_iota(jnp.int32, (2 * node_dev, ROW), 0).astype(F32)

    for copy in meta_copies:
        copy.wait_recv()

    def build(step, carry):
        level = step // (owners // 2)
        duo = lax.rem(step, owners // 2)
        codes = []
        for a in range(2):
            child = tables[2 * duo + a, level, 0:1, :]
            codes.append(tables[2 * duo + a, level, 1:2, :])
            weight = tables[2 * duo + a, level, 2:3, :]
            q = tables[2 * duo + a, level, 3:4, :]
            hot = child_iota == child + float(a * node_dev)
            g1h, g1l = halves(jnp.where(hot, weight * q, 0.0))
            g2h, g2l = halves(jnp.where(hot, weight * (1.0 - q) * 0.25, 0.0))
            columns = slice(a * ROW, (a + 1) * ROW)
            for n, piece in enumerate((g1h, g1l, g2h, g2l)):
                gmat[n * SIDE : (n + 1) * SIDE, columns] = piece
        code = jnp.concatenate(codes, axis=1)

        for part in range(2 * nodes // SIDE):
            rows = slice(part * SIDE, (part + 1) * SIDE)
            wide = jnp.concatenate([numbers[rows, :]] * 4, axis=1)
            picks[duo, rows, :] = jnp.where(wide == code, 1.0, 0.0).astype(BF16)
        where_to = pl.ds(pl.multiple_of(duo * SIDE, SIDE), SIDE)
        for r in range(2):
            rows = slice(r * nodes, (r + 1) * nodes)
            found = mm_nt(picks[duo, rows, :], gmat[0 : 2 * SIDE, :])
            hi, lo = halves(found[:, :SIDE] + found[:, SIDE:])
            m1h[level, rows, where_to] = hi
            m1l[level, rows, where_to] = lo
            found = mm_nt(picks[duo, rows, :], gmat[2 * SIDE : 4 * SIDE, :])
            hi, lo = halves(found[:, :SIDE] + found[:, SIDE:])
            m2h[level, rows, where_to] = hi
            m2l[level, rows, where_to] = lo
        return carry

    lax.fori_loop(0, levels * (owners // 2), build, 0)

    times = jnp.zeros((nodes, SIDE), F32)
    for i in range(owners):
        wanted = jnp.where(topo_lane, tables[i, levels - 1, 0:1, SIDE:], -1.0)
        times += jnp.where(numbers[0:nodes, :] == wanted, 1.0, 0.0)
    mult[...] = jnp.broadcast_to(jnp.sum(times, axis=1, keepdims=True), (nodes, SIDE))

    def over_states(x):
        total = x[:, :SIDE]
        for k in range(1, states):
            total = total + x[:, k * SIDE : (k + 1) * SIDE]
        return total

    def advance(level, slot, first, last, fresh):
        inner = slice(first, last)
        for r in range(2):
            rows = slice(r * nodes, (r + 1) * nodes)
            bh = m2h[level, rows, inner]
            flat = mm(bh, sums[slot, inner, :])
            flat = flat[:, :SIDE] + flat[:, SIDE:]
            flat = flat + mm(m2l[level, rows, inner], sums[slot, inner, :SIDE])
            flat = jnp.concatenate([flat, flat], axis=1)
            for n in range(states // 2):
                cols = slice(n * ROW, (n + 1) * ROW)
                full = mm(m1h[level, rows, inner], ch[slot, inner, cols])
                full = full + mm(m1h[level, rows, inner], cl[slot, inner, cols])
                full = full + mm(m1l[level, rows, inner], ch[slot, inner, cols])
                full = full + flat
                if not fresh:
                    full = full + pair[rows, cols]
                pair[rows, cols] = full

    own_leaf.wait()
    half = owners // 2
    for part in range(2):
        for i in range(part * half, (part + 1) * half):
            if i:
                leaf_copies[i - 1].wait_recv()
            block = inbox[i]
            rows = slice(i * node_dev, (i + 1) * node_dev)
            total = None
            for k in range(states):
                x = block[:, k, :]
                total = x if k == 0 else total + x
                cols = slice(k * SIDE, (k + 1) * SIDE)
                ch[0, rows, cols], cl[0, rows, cols] = halves(x)
            sums[0, rows, :SIDE], sums[0, rows, SIDE:] = halves(total)
        advance(0, 0, part * half * node_dev, (part + 1) * half * node_dev, part == 0)

    def multiply(slot):
        for step in range(nodes // SIDE):
            rows = slice(step * SIDE, (step + 1) * SIDE)
            other = slice(nodes + step * SIDE, nodes + (step + 1) * SIDE)
            x = pair[rows, :] * pair[other, :]
            ch[slot, rows, :], cl[slot, rows, :] = halves(x)
            sums[slot, rows, :SIDE], sums[slot, rows, SIDE:] = halves(over_states(x))

    slot = 0
    for level in range(1, levels):
        slot = level % 2
        multiply(slot)
        advance(level, slot, 0, nodes, True)

    site_row = lax.broadcasted_iota(jnp.int32, counts.shape, 0)
    count = jnp.sum(
        jnp.where(site_row == me, counts[...].astype(F32) / sites_all, 0.0), axis=0, keepdims=True
    )
    picked = [jnp.zeros((1, SIDE), F32)] * owners
    for first in range(0, nodes, SIDE):
        rows = slice(first, first + SIDE)
        p0 = pair[rows, :]
        p1 = pair[nodes + first : nodes + first + SIDE, :]
        lik = 0.25 * over_states(p0 * p1)
        score = jnp.sum(count * jnp.log(lik), axis=1, keepdims=True)
        here = numbers[rows, :]
        for i in range(owners):
            wanted = jnp.where(topo_lane, tables[i, levels - 1, 0:1, SIDE:], -1.0)
            picked[i] = picked[i] + jnp.sum(
                jnp.where(here == wanted, score, 0.0), axis=0, keepdims=True
            )
        factor = count * 0.25 / lik * mult[rows, :]
        wide = jnp.concatenate([factor] * states, axis=1)
        for r in range(2):
            adj = (p0 if r else p1) * wide
            to = slice(r * nodes + first, r * nodes + first + SIDE)
            ahi[to, :], alo[to, :] = halves(adj)
            adj_sums[to, :SIDE], adj_sums[to, SIDE:] = halves(over_states(adj))

    for step in range(2 * nodes // ROW):
        cols = slice(step * ROW, (step + 1) * ROW)
        ah, al = ahi[cols, :], alo[cols, :]
        both = adj_sums[cols, :]
        d1 = mm_nt(ch[slot], ah) + mm_nt(ch[slot], al) + mm_nt(cl[slot], ah)
        turned = jnp.concatenate([both[:, SIDE:], both[:, :SIDE]], axis=1)
        d2 = mm_nt(sums[slot], both) + mm_nt(sums[slot], turned)
        d1h, d1l = halves(d1)
        d2h, d2l = halves(d2)
        for i in range(owners):
            rows = slice(i * node_dev, (i + 1) * node_dev)
            for n, piece in enumerate((d1h, d1l, d2h, d2l)):
                dst[i, n * node_dev : (n + 1) * node_dev, cols] = piece[rows, :]

    edge_iota = lax.broadcasted_iota(jnp.int32, (node_dev, ROW), 0).astype(F32)
    last = levels - 1
    first_copies = []
    for step in range(owners):
        i = (step + 1) % owners
        found = mm(dst[i], picks[i // 2, :, (i % 2) * ROW : (i % 2 + 1) * ROW])
        hot = edge_iota == tables[i, last, 0:1, :]
        d1 = found[:node_dev] + found[node_dev : 2 * node_dev]
        d2 = found[2 * node_dev : 3 * node_dev] + found[3 * node_dev :]
        q = tables[i, last, 3:4, :]
        mixed = jnp.where(hot, q * d1 + (1.0 - q) * 0.25 * d2, 0.0)
        grads = jnp.sum(mixed, axis=0, keepdims=True)
        grads = grads + jnp.concatenate([jnp.zeros((1, SIDE), F32), picked[i]], axis=1)
        send1[i] = jnp.broadcast_to(grads, (8, ROW))
        if i == 0:
            continue
        copy = pltpu.make_async_remote_copy(
            src_ref=send1.at[i],
            dst_ref=recv1.at[i],
            send_sem=r1_send.at[i],
            recv_sem=r1_recv.at[i],
            device_id={"node": lax.rem(me - i + owners, owners)},
            device_id_type=MESH,
        )
        copy.start()
        first_copies.append(copy)
    total = send1[0]
    for i in range(1, owners):
        first_copies[i - 1].wait_recv()
        total = total + recv1[i]
    send2[...] = total
    recv2[my_site] = total
    second_copies = []
    for i in range(1, site_ways):
        copy = pltpu.make_async_remote_copy(
            src_ref=send2,
            dst_ref=recv2.at[my_site],
            send_sem=r2_send.at[i],
            recv_sem=r2_recv.at[i],
            device_id={"site": lax.rem(my_site + i, site_ways)},
            device_id_type=MESH,
        )
        copy.start()
        second_copies.append(copy)
    for copy in meta_copies + leaf_copies + first_copies:
        copy.wait_send()
    for copy in second_copies:
        copy.wait_recv()
    total = recv2[0]
    for i in range(1, site_ways):
        total = total + recv2[i]
    grad_out[...] = total[0, 0:edge_dev]
    tail = total[0:1, SIDE:]
    which = (lane - SIDE // 2) // topo_shape[1]
    here = jnp.zeros((1, SIDE), F32)
    for t in range(topo_shape[0]):
        mine = topo_lane & (which == t)
        score = jnp.sum(jnp.where(mine, tail, 0.0), axis=1, keepdims=True)
        here = here + jnp.where(lane == t, score, 0.0)
    loglik_out[...] = here[0, 0 : topo_shape[0]]
    for copy in second_copies:
        copy.wait_send()


def by_sites(leaf_partials, dag_edges, weights, lengths, counts, topo_nodes):
    node_dev, states, site_dev = leaf_partials.shape
    levels, edge_dev, _ = dag_edges.shape
    owners, site_ways = lax.axis_size("node"), lax.axis_size("site")
    nodes = owners * node_dev
    wide = states * SIDE
    far = pl.BlockSpec(memory_space=pltpu.HBM)
    near = pl.BlockSpec(memory_space=pltpu.VMEM)
    operator = pltpu.VMEM((levels, 2 * nodes, nodes), BF16)
    loglik, grads = pl.pallas_call(
        functools.partial(
            kernel,
            (
                owners,
                site_ways,
                node_dev,
                states,
                levels,
                topo_nodes.shape,
                site_dev * site_ways,
            ),
        ),
        out_shape=(
            jax.ShapeDtypeStruct((topo_nodes.shape[0],), F32),
            jax.ShapeDtypeStruct((edge_dev,), F32),
        ),
        in_specs=[far] * 6,
        out_specs=(near, near),
        scratch_shapes=[
            pltpu.VMEM((levels, 3, edge_dev), jnp.int32),
            pltpu.VMEM((levels, edge_dev), F32),
            pltpu.VMEM((levels, edge_dev), F32),
            pltpu.VMEM((owners, SIDE), jnp.int32),
            pltpu.VMEM(topo_nodes.shape, jnp.int32),
            pltpu.VMEM((levels, 4, ROW), F32),
            pltpu.VMEM((owners, node_dev, states, SIDE), F32),
            pltpu.VMEM((owners, levels, 4, ROW), F32),
            operator,
            operator,
            operator,
            operator,
            pltpu.VMEM((owners // 2, 2 * nodes, 2 * ROW), BF16),
            pltpu.VMEM((4 * SIDE, 2 * ROW), BF16),
            pltpu.VMEM((2, nodes, wide), BF16),
            pltpu.VMEM((2, nodes, wide), BF16),
            pltpu.VMEM((2, nodes, 2 * SIDE), BF16),
            pltpu.VMEM((2 * nodes, wide), F32),
            pltpu.VMEM((nodes, SIDE), F32),
            pltpu.VMEM((2 * nodes, wide), BF16),
            pltpu.VMEM((2 * nodes, wide), BF16),
            pltpu.VMEM((2 * nodes, 2 * SIDE), BF16),
            pltpu.VMEM((owners, 4 * node_dev, 2 * nodes), BF16),
            pltpu.VMEM((2 * nodes, SIDE), F32),
            pltpu.VMEM((nodes, SIDE), F32),
            pltpu.VMEM((owners, 8, ROW), F32),
            pltpu.VMEM((owners, 8, ROW), F32),
            pltpu.VMEM((8, ROW), F32),
            pltpu.VMEM((site_ways, 8, ROW), F32),
            pltpu.SemaphoreType.DMA((owners,)),
            pltpu.SemaphoreType.DMA((owners,)),
            pltpu.SemaphoreType.DMA((owners,)),
            pltpu.SemaphoreType.DMA((owners,)),
            pltpu.SemaphoreType.DMA((6,)),
            pltpu.SemaphoreType.DMA((owners,)),
            pltpu.SemaphoreType.DMA((owners,)),
            pltpu.SemaphoreType.DMA((site_ways,)),
            pltpu.SemaphoreType.DMA((site_ways,)),
        ],
        compiler_params=pltpu.CompilerParams(
            collective_id=0, has_side_effects=True, vmem_limit_bytes=64 * 2**20
        ),
    )(
        leaf_partials,
        jnp.transpose(dag_edges, (0, 2, 1)),
        weights,
        lengths,
        counts.reshape(owners, SIDE),
        topo_nodes,
    )
    return loglik, grads


def either(leaf_partials, dag_edges, weights, lengths, counts, topo_nodes):
    node_dev, states, site_dev = leaf_partials.shape
    owners = lax.axis_size("node")
    fits = (
        site_dev == owners * SIDE
        and 2 * node_dev == SIDE
        and owners % 2 == 0
        and owners <= 8
        and dag_edges.shape[1] == ROW * 3 // 4
        and topo_nodes.size <= ROW // 4
    )
    form = by_sites if fits else on_device
    return form(leaf_partials, dag_edges, weights, lengths, counts, topo_nodes)


def solution(mesh):
    return jax.shard_map(
        either,
        mesh=mesh,
        in_specs=(
            P("node", None, "site"),
            P(None, "node", None),
            P(None, "node"),
            P(None, "node"),
            P("site"),
            P("node", None),
        ),
        out_specs=(P("node"), P("node")),
        check_vma=False,
    )
```
